256 devices in a mesh: space: 64 (over x, y_lo, z), modes: 4 (over y_hi, core).
Axes of the slice: x: 4, y: 4 (y_hi: 2, y_lo: 2; y = y_hi * 2 + y_lo), z: 8, core: 2. Of those that a mesh axis runs over, the one named last changes fastest.
Arguments:
- pressure: float32 [256, 1024, 512], P('modes', 'space'), may hold values from -6 to 6
- gap_terms: float32 [8, 1024, 512], P(None, 'space'), may hold values from 0.05 to 0.5
- coupling: float32 [8, 256, 256], replicated, may hold values from -0.1875 to 0.1875
- pattern: int32 [8, 4, 4], replicated, may hold values 0 or 1
Outputs:
- damped: float32 [256, 1024, 512], P('modes', 'space')
The draws below stay inside these ranges and needn't reach their ends.
All inputs are finite; a program needn't handle non-finite values.
Results may differ from the reference program's by a relative error of at most 0.0001.
Values sent between devices are 32-bit elements; how exact they have to be, the bound alone decides.
A program may use at most 128 MiB of HBM per device.

```python
import math
import jax
import jax.numpy as jnp
from jax import lax

P_SIZE = 256
K = 8
BLOCK = 64
NY = 512
NB = 4
NX = 1024


def touch_ends(drawn, stream_key, low, top_value):
    shape = drawn.shape
    place = [jax.random.randint(jax.random.fold_in(stream_key, axis), (), 0, shape[axis]) for axis in range(len(shape))]
    drawn = drawn.at[tuple(place)].set(low)
    longest = shape.index(max(shape))
    place[longest] = (place[longest] + 1) % shape[longest]
    return drawn.at[tuple(place)].set(top_value)


def steps_of(own_key, dims, pieces, low, top_value):
    def one(position, parts):
        steps = jax.random.uniform(jax.random.fold_in(jax.random.fold_in(own_key, 6), position), (parts,), jnp.float32, low / len(pieces), top_value / len(pieces))
        return jnp.repeat(jnp.exp(steps), dims[position] // parts).reshape((-1,) + (1,) * (len(dims) - position - 1))

    factor_of = one(*pieces[0])
    for cut in pieces[1:]:
        factor_of = factor_of * one(*cut)
    return factor_of


def centred(rng, dims, spread, bound, cuts=(), held_as=jnp.bfloat16):
    level = steps_of(rng, dims, cuts, -0.22, 0.18) if cuts else 1.0
    values = jax.random.normal(rng, dims, jnp.float32) * spread * level
    return jnp.minimum(jnp.maximum(values, -bound), bound).astype(held_as)


def setup_inputs(seed: int = 0) -> dict:
    splits = jax.random.split(jax.random.key(seed), 5)
    pressure = centred(splits[0], (P_SIZE, NX, NY), 1.0, 6.0, ((0, 4), (1, 64)), jnp.float32)
    gap_terms = jnp.clip(jnp.exp(math.log(0.5) - 2.3025851 * jax.random.uniform(splits[1], (K, NX, NY), jnp.float32) ** steps_of(splits[1], (K, NX, NY), ((1, 64),), -0.2, 0.2)), 0.05, 0.5)
    coupling = centred(splits[2], (K, P_SIZE, P_SIZE), (K * P_SIZE // 2) ** -0.5, 0.1875, (), jnp.float32)
    pattern = touch_ends((jax.random.randint(splits[3], (K, NB, NB), 0, 2) < 1).astype(jnp.int32), jax.random.fold_in(splits[3], 1), 0, 1)
    return dict(pressure=pressure, gap_terms=gap_terms, coupling=coupling, pattern=pattern)


def faces(pext, cext):
    center = cext[1:-1, 1:-1]
    inner = pext[:, 1:-1, 1:-1]
    total = (0.5 * (center + cext[:-2, 1:-1])) * (inner - pext[:, :-2, 1:-1])
    total = total + (0.5 * (center + cext[2:, 1:-1])) * (inner - pext[:, 2:, 1:-1])
    total = total + (0.5 * (center + cext[1:-1, :-2])) * (inner - pext[:, 1:-1, :-2])
    total = total + (0.5 * (center + cext[1:-1, 2:])) * (inner - pext[:, 1:-1, 2:])
    return total


def operate(field, coef):
    pext = jnp.pad(field, ((0, 0), (1, 1), (1, 1)))
    cext = jnp.pad(coef, 1, mode="edge")
    return faces(pext, cext)


def galerkin(field, gap_terms, mixing):
    modes_all = field.shape[0]
    total = jnp.zeros(field.shape, jnp.float32)
    for k in range(K):
        mixed = jnp.dot(mixing[k], field.reshape(modes_all, -1), precision=lax.Precision.HIGHEST, preferred_element_type=jnp.float32).reshape(field.shape)
        total = total + operate(mixed, gap_terms[k])
    return total


def reference(pressure, gap_terms, coupling, pattern):
    expand = jnp.repeat(jnp.repeat(pattern.astype(jnp.float32), BLOCK, axis=1), BLOCK, axis=2)
    mixing = coupling * expand
    first = galerkin(pressure, gap_terms, mixing)
    return galerkin(first, gap_terms, mixing)
```

```python
import jax
import jax.numpy as jnp
from jax import lax
from jax.experimental import pallas as pl
from jax.experimental.pallas import tpu as pltpu
from jax.sharding import PartitionSpec as P

MESH = pl.DeviceIdType.MESH
K = 8
MODES = 256
BLOCK = 64
ROWS = 16
LANES = 128
ZRUN = 8
GROUPS = MODES // 16
CHUNKS = 6
F32 = jnp.float32
BF16 = jnp.bfloat16


def lane_iota(rows):
    return lax.broadcasted_iota(jnp.int32, (rows, LANES), 1)


def split(value):
    high = value.astype(BF16)
    return high, (value - high.astype(F32)).astype(BF16)


def kernel(
    press, gap, coupling, pattern, out,
    strip, gap_in, coup, rows_v, first, extra, extra1, extra_own, damp, home, sendrows,
    gap_pad, c_right, c_left, c_down, e_coef, mix_hi, mix_lo, x_hi, x_lo, halo_out, halo_in,
    load_sem, in_send, in_recv, z_send, z_recv, out_send, out_recv, store_sem,
):
    space = lax.axis_index("space")
    mode = lax.axis_index("modes")
    count = lax.axis_size("space")
    y_lo = lax.rem(lax.div(space, ZRUN), 2)

    def swapped(index, bit):
        return index + bit * (lax.rem(index, 2) * 2 + lax.div(index, 2) - index)

    quarter = swapped(mode, y_lo)
    hi, core = lax.div(mode, 2), lax.rem(mode, 2)
    group = [(1 - hi) * 2 + core, (1 - hi) * 2 + 1 - core, hi * 2 + 1 - core]
    group_quarter = [swapped(peer, y_lo) for peer in group]

    def beside(step):
        other = lax.rem(space + step + count, count)
        other_y = lax.rem(lax.div(other, ZRUN), 2)
        return (other, swapped(quarter, other_y))

    before, after = beside(-1), beside(1)

    def columns(t):
        return slice(t * LANES, (t + 1) * LANES)

    press_loads = [pltpu.make_async_copy(press.at[:, columns(t)], strip.at[t], load_sem.at[t]) for t in range(4)]
    gap_loads = [pltpu.make_async_copy(gap.at[:, columns(t)], gap_in.at[t], load_sem.at[4 + t]) for t in range(4)]
    coup_load = pltpu.make_async_copy(coupling, coup, load_sem.at[8])
    for load in press_loads + gap_loads + [coup_load]:
        load.start()

    barrier = pltpu.get_barrier_semaphore()
    for peer in group:
        pl.semaphore_signal(barrier, inc=1, device_id=(space, peer), device_id_type=MESH)
    for peer in (before, after):
        pl.semaphore_signal(barrier, inc=1, device_id=peer, device_id_type=MESH)

    for load in gap_loads:
        load.wait()
    for r in range(ROWS):
        slabs = [gap_in[t, pl.ds(r, K, stride=ROWS), :] for t in range(4)]
        slabs = [jnp.broadcast_to(slabs[0][:, :1], (K, LANES)), *slabs, jnp.broadcast_to(slabs[3][:, LANES - 1 :], (K, LANES))]
        for t in range(6):
            gap_pad[r + 2, :, columns(t)] = slabs[t]

    for load in press_loads:
        load.wait()

    def own_rows(r):
        for t in range(4):
            sendrows[t, r] = strip[t, pl.ds(r, BLOCK, stride=ROWS), :]

    for r in (0, 1, 14, 15):
        own_rows(r)

    pl.semaphore_wait(barrier, 5)

    mine = pl.multiple_of(mode * BLOCK, BLOCK)

    def row_copy(peer, peer_quarter, row, rows, slot, source):
        return pltpu.make_async_remote_copy(
            src_ref=sendrows.at[peer_quarter, pl.ds(row, rows)],
            dst_ref=rows_v.at[pl.ds(row + 2, rows), pl.ds(pl.multiple_of(source * BLOCK, BLOCK), BLOCK)],
            send_sem=in_send.at[slot, peer],
            recv_sem=in_recv.at[slot, source],
            device_id=(space, peer),
            device_id_type=MESH,
        )

    def extra_copy(peer, peer_quarter, source):
        return pltpu.make_async_remote_copy(
            src_ref=extra_own.at[peer_quarter],
            dst_ref=extra.at[pl.ds(pl.multiple_of(source * BLOCK, BLOCK), BLOCK)],
            send_sem=in_send.at[CHUNKS + 2, peer],
            recv_sem=in_recv.at[CHUNKS + 2, source],
            device_id=(space, peer),
            device_id_type=MESH,
        )

    for row, slot in ((0, CHUNKS), (14, CHUNKS + 1)):
        for peer, peer_quarter in zip(group, group_quarter):
            row_copy(peer, peer_quarter, row, 2, slot, mode).start()

    def z_copy(source, target, slot, device):
        return pltpu.make_async_remote_copy(
            src_ref=source, dst_ref=target, send_sem=z_send.at[slot], recv_sem=z_recv.at[slot],
            device_id=device, device_id_type=MESH,
        )

    gap_copies = [
        z_copy(gap_pad.at[pl.ds(2, 2)], gap_pad.at[pl.ds(ROWS + 2, 2)], 0, before),
        z_copy(gap_pad.at[pl.ds(ROWS, 2)], gap_pad.at[pl.ds(0, 2)], 1, after),
    ]
    for copy in gap_copies:
        copy.start()

    for r in range(2, 14):
        own_rows(r)

    def own_extra(g, carry):
        at = pl.ds(pl.multiple_of(g * 8, 8), 8)
        lane = lane_iota(8)
        built = [jnp.zeros((8, LANES), F32) for _ in range(4)]
        for r in range(ROWS):
            rolled = [pltpu.roll(sendrows[t, r, at, :], 2, 1) for t in range(4)]
            edges = [jnp.where(lane < 2, 0.0, rolled[0])]
            edges += [jnp.where(lane < 2, rolled[b - 1], rolled[b]) for b in range(1, 4)]
            edges.append(jnp.where(lane < 2, rolled[3], 0.0))
            start = 6 * (r + 2)
            for t in range(4):
                both = jnp.where(lane < 3, edges[t], pltpu.roll(edges[t + 1], 2, 1))
                inside = (lane >= start) & (lane < start + 6)
                built[t] = jnp.where(inside, pltpu.roll(both, start, 1), built[t])
        for t in range(4):
            extra_own[t, at, :] = built[t]
        return carry

    lax.fori_loop(0, BLOCK // 8, own_extra, 0)
    for peer, peer_quarter in zip(group, group_quarter):
        extra_copy(peer, peer_quarter, mode).start()

    for c in range(CHUNKS):
        for peer, peer_quarter in zip(group, group_quarter):
            row_copy(peer, peer_quarter, 2 * c + 2, 2, c, mode).start()

    extra[pl.ds(mine, BLOCK), :] = extra_own[quarter]
    for r in range(ROWS):
        rows_v[r + 2, pl.ds(mine, BLOCK), :] = sendrows[quarter, r]

    coup_load.wait()
    wide = lax.broadcasted_iota(jnp.int32, (BLOCK, MODES), 1)
    for k in range(K):
        for b in range(4):
            scale = [pattern[k, b, c].astype(F32) for c in range(4)]
            factor = jnp.where(
                wide < 128,
                jnp.where(wide < 64, scale[0], scale[1]),
                jnp.where(wide < 192, scale[2], scale[3]),
            )
            high, low = split(coup[k, b * BLOCK : (b + 1) * BLOCK, :] * factor)
            mix_hi[b * BLOCK : (b + 1) * BLOCK, k * MODES : (k + 1) * MODES] = high
            mix_lo[b * BLOCK : (b + 1) * BLOCK, k * MODES : (k + 1) * MODES] = low

    for copy in gap_copies:
        copy.wait_recv()

    @pl.when(space == 0)
    def _():
        gap_pad[1] = gap_pad[2]

    @pl.when(space == count - 1)
    def _():
        gap_pad[ROWS + 2] = gap_pad[ROWS + 1]

    def tile(index, side):
        return gap_pad[index, :, pl.ds(pl.multiple_of((quarter + side) * LANES, LANES), LANES)]

    lane8 = lane_iota(8)

    def coefficients(index, slab):
        left, here, right = tile(index, 0), tile(index, 1), tile(index, 2)
        below = tile(jnp.minimum(index + 1, ROWS + 3), 1)
        next_cell = jnp.where(lane8 == LANES - 1, pltpu.roll(right, LANES - 1, 1), pltpu.roll(here, LANES - 1, 1))
        last_cell = jnp.where(lane8 == 0, pltpu.roll(left, 1, 1), pltpu.roll(here, 1, 1))
        for ref, value in ((c_right, next_cell), (c_left, last_cell), (c_down, below)):
            face = 0.5 * (here + value)
            for k in range(K):
                ref[index, k] = jnp.broadcast_to(face[k : k + 1, :], (8, LANES))
        edge_left = jnp.where(lane8 < 2, pltpu.roll(left, 2, 1), pltpu.roll(here, 2, 1))
        edge_right = jnp.where(lane8 < 2, pltpu.roll(here, 2, 1), pltpu.roll(right, 2, 1))
        both = jnp.where(lane8 < 3, edge_left, pltpu.roll(edge_right, 2, 1))
        start = 6 * index
        return jnp.where((lane8 >= start) & (lane8 < start + 6), pltpu.roll(both, start, 1), slab)

    slab = lax.fori_loop(0, ROWS + 4, coefficients, jnp.zeros((8, LANES), F32))
    for n, shift in enumerate((LANES - 1, 1, LANES - 6, 6)):
        face = 0.5 * (slab + pltpu.roll(slab, shift, 1))
        for k in range(K):
            e_coef[n, k] = jnp.broadcast_to(face[k : k + 1, :], (8, LANES))

    for slot, row in ((CHUNKS, 0), (CHUNKS + 1, 14)):
        for peer in group:
            row_copy(peer, 0, row, 2, slot, peer).wait_recv()
    for peer in group:
        extra_copy(peer, 0, peer).wait_recv()

    lane32 = lane_iota(32)
    for n, shift in enumerate((LANES - 12, 32)):
        packed = jnp.zeros((32, LANES), F32)
        for g in range(8):
            moved = pltpu.roll(extra[32 * g : 32 * g + 32, :], (shift + 16 * g) % LANES, 1)
            packed = jnp.where((lane32 >= 16 * g) & (lane32 < 16 * g + 16), moved, packed)
        halo_out[n] = packed

    edge_copies = [
        z_copy(halo_out.at[0], halo_in.at[1], 2, before),
        z_copy(halo_out.at[1], halo_in.at[0], 3, after),
        z_copy(rows_v.at[pl.ds(2, 2)], rows_v.at[pl.ds(ROWS + 2, 2)], 4, before),
        z_copy(rows_v.at[pl.ds(ROWS, 2)], rows_v.at[pl.ds(0, 2)], 5, after),
    ]
    for copy in edge_copies:
        copy.start()
    for copy in edge_copies:
        copy.wait_recv()

    top, bottom = space == 0, space == count - 1

    @pl.when(top)
    def _():
        rows_v[0:2] = jnp.zeros((2, MODES, LANES), F32)

    @pl.when(bottom)
    def _():
        rows_v[ROWS + 2 :] = jnp.zeros((2, MODES, LANES), F32)

    upper = jnp.where(top, 0.0, halo_in[0])
    lower = jnp.where(bottom, 0.0, halo_in[1])
    for g in range(8):
        at = slice(32 * g, 32 * g + 32)
        value = jnp.where(lane32 < 12, pltpu.roll(upper, (LANES - 16 * g) % LANES, 1), extra[at, :])
        inside = (lane32 >= 108) & (lane32 < 120)
        extra[at, :] = jnp.where(inside, pltpu.roll(lower, (108 - 16 * g) % LANES, 1), value)

    def twice(value):
        return jnp.concatenate([value, value], axis=0)

    def put(k, g, column, value):
        high, low = split(value)
        at = pl.ds(pl.multiple_of(k * MODES + g * 16, 16), 16)
        x_hi[at, column : column + LANES] = high
        x_lo[at, column : column + LANES] = low

    def product(width):
        return (
            jnp.dot(mix_hi[...], x_hi[:, :width], preferred_element_type=F32)
            + jnp.dot(mix_hi[...], x_lo[:, :width], preferred_element_type=F32)
            + jnp.dot(mix_lo[...], x_hi[:, :width], preferred_element_type=F32)
        )

    def extra_terms(g, carry):
        v = extra[pl.ds(pl.multiple_of(g * 16, 16), 16), :]
        diffs = [v - pltpu.roll(v, shift, 1) for shift in (LANES - 1, 1, LANES - 6, 6)]
        for k in range(K):
            total = twice(e_coef[0, k]) * diffs[0]
            for n in range(1, 4):
                total = total + twice(e_coef[n, k]) * diffs[n]
            put(k, g, 0, total)
        return carry

    lax.fori_loop(0, GROUPS, extra_terms, 0)
    column = lax.rem(lane_iota(MODES), 6)
    outside = ((column == 1) & (quarter == 0)) | ((column == 4) & (quarter == 3))
    extra1[...] = jnp.where(outside, 0.0, product(LANES))

    lane16 = lane_iota(16)

    def terms(source, base, sides, index):
        def body(g, carry):
            at = pl.ds(pl.multiple_of(g * 16, 16), 16)
            v = [source[base + n, at, :] for n in range(4)]
            side = sides[at, :]
            down = [v[n] - v[n + 1] for n in range(3)]
            diffs = []
            for n in range(2):
                here = v[n + 1]
                lane = 6 * (index + n)
                left = jnp.where(lane16 == 0, pltpu.roll(side, LANES - 1 - lane, 1), pltpu.roll(here, 1, 1))
                right = jnp.where(
                    lane16 == LANES - 1, pltpu.roll(side, LANES - 5 - lane, 1), pltpu.roll(here, LANES - 1, 1)
                )
                diffs.append((here - left, here - right))
            for k in range(K):
                flux = [twice(c_down[index - 1 + n, k]) * down[n] for n in range(3)]
                for n in range(2):
                    total = twice(c_left[index + n, k]) * diffs[n][0] + twice(c_right[index + n, k]) * diffs[n][1]
                    put(k, g, n * LANES, total + (flux[n + 1] - flux[n]))
            return carry

        lax.fori_loop(0, GROUPS, body, 0)

    def home_copy(peer, owner_of_block, pair, their_quarter):
        return pltpu.make_async_remote_copy(
            src_ref=damp.at[pl.ds(2 * pair, 2), pl.ds(pl.multiple_of(owner_of_block * BLOCK, BLOCK), BLOCK)],
            dst_ref=home.at[their_quarter, pl.ds(2 * pair, 2)],
            send_sem=out_send.at[pair, peer],
            recv_sem=out_recv.at[pair, their_quarter],
            device_id=(space, peer),
            device_id_type=MESH,
        )

    def step(i, carry):
        @pl.when((i >= 1) & (i <= CHUNKS))
        def _():
            for peer in group:
                row_copy(peer, 0, 2 * i, 2, i - 1, peer).wait_recv()

        terms(rows_v, 2 * i, extra, 2 * i + 1)
        result = product(2 * LANES)
        first[2 * i] = jnp.where(top & (i == 0), 0.0, result[:, :LANES])
        first[2 * i + 1] = jnp.where(bottom & (i == ROWS // 2), 0.0, result[:, LANES:])

        @pl.when(i >= 1)
        def _():
            j = i - 1
            terms(first, 2 * j, extra1, 2 * j + 2)
            result = product(2 * LANES)
            damp[2 * j] = result[:, :LANES]
            damp[2 * j + 1] = result[:, LANES:]
            for peer in group:
                home_copy(peer, peer, j, quarter).start()

        return carry

    lax.fori_loop(0, ROWS // 2 + 1, step, 0)

    for pair in range(ROWS // 2):
        for peer, peer_quarter in zip(group, group_quarter):
            home_copy(peer, mode, pair, peer_quarter).wait_recv()
        for r in (2 * pair, 2 * pair + 1):
            home[quarter, r] = damp[r, pl.ds(mine, BLOCK), :]
            for t in range(4):
                strip[t, pl.ds(r, BLOCK, stride=ROWS), :] = home[t, r]
    stores = [pltpu.make_async_copy(strip.at[t], out.at[:, columns(t)], store_sem.at[t]) for t in range(4)]
    for store in stores:
        store.start()

    for slot, row in [(c, 2 * c + 2) for c in range(CHUNKS)] + [(CHUNKS, 0), (CHUNKS + 1, 14)]:
        for peer in group:
            row_copy(peer, 0, row, 2, slot, mode).wait_send()
    for peer in group:
        extra_copy(peer, 0, mode).wait_send()
        for pair in range(ROWS // 2):
            home_copy(peer, peer, pair, quarter).wait_send()
    for copy in gap_copies + edge_copies:
        copy.wait_send()
    for store in stores:
        store.wait()


def per_device(pressure, gap_terms, coupling, pattern):
    cells = pressure.shape[2]
    vmem = pltpu.VMEM
    result = pl.pallas_call(
        kernel,
        out_shape=jax.ShapeDtypeStruct((BLOCK * ROWS, cells), F32),
        in_specs=[
            pl.BlockSpec(memory_space=pl.ANY),
            pl.BlockSpec(memory_space=pl.ANY),
            pl.BlockSpec(memory_space=pl.ANY),
            pl.BlockSpec(memory_space=pltpu.SMEM),
        ],
        out_specs=pl.BlockSpec(memory_space=pl.ANY),
        scratch_shapes=[
            vmem((4, BLOCK * ROWS, LANES), F32),
            vmem((4, K * ROWS, LANES), F32),
            vmem((K, MODES, MODES), F32),
            vmem((ROWS + 4, MODES, LANES), F32),
            vmem((ROWS + 2, MODES, LANES), F32),
            vmem((MODES, LANES), F32),
            vmem((MODES, LANES), F32),
            vmem((4, BLOCK, LANES), F32),
            vmem((ROWS, MODES, LANES), F32),
            vmem((4, ROWS, BLOCK, LANES), F32),
            vmem((4, ROWS, BLOCK, LANES), F32),
            vmem((ROWS + 4, K, cells + 2 * LANES), F32),
            vmem((ROWS + 4, K, 8, LANES), F32),
            vmem((ROWS + 4, K, 8, LANES), F32),
            vmem((ROWS + 4, K, 8, LANES), F32),
            vmem((4, K, 8, LANES), F32),
            vmem((MODES, K * MODES), BF16),
            vmem((MODES, K * MODES), BF16),
            vmem((K * MODES, 2 * LANES), BF16),
            vmem((K * MODES, 2 * LANES), BF16),
            vmem((2, 32, LANES), F32),
            vmem((2, 32, LANES), F32),
            pltpu.SemaphoreType.DMA((9,)),
            pltpu.SemaphoreType.DMA((CHUNKS + 3, 4)),
            pltpu.SemaphoreType.DMA((CHUNKS + 3, 4)),
            pltpu.SemaphoreType.DMA((6,)),
            pltpu.SemaphoreType.DMA((6,)),
            pltpu.SemaphoreType.DMA((ROWS // 2, 4)),
            pltpu.SemaphoreType.DMA((ROWS // 2, 4)),
            pltpu.SemaphoreType.DMA((4,)),
        ],
        compiler_params=pltpu.CompilerParams(
            collective_id=0, has_side_effects=True, vmem_limit_bytes=56 * 1024 * 1024
        ),
        cost_estimate=pl.CostEstimate(flops=26_000_000_000, bytes_accessed=7_000_000, transcendentals=0),
        name="galerkin_twice",
    )(pressure.reshape(BLOCK * ROWS, cells), gap_terms.reshape(K * ROWS, cells), coupling, pattern)
    return result.reshape(pressure.shape)


def solution(mesh):
    placed = (P("modes", "space", None), P(None, "space", None), P(), P())
    return jax.shard_map(
        per_device, mesh=mesh, in_specs=placed, out_specs=P("modes", "space", None), check_vma=False
    )
```

```python
import jax
import jax.numpy as jnp
from jax import lax
from jax.experimental import pallas as pl
from jax.experimental.pallas import tpu as pltpu
from jax.sharding import PartitionSpec as P

MESH = pl.DeviceIdType.MESH
K = 8
MODES = 256
BLOCK = 64
ROWS = 16
LANES = 128
ZRUN = 8
GROUPS = MODES // 16
CHUNKS = 6
FIRST = ROWS + 4
DAMPED = 2 * ROWS + 6
F32 = jnp.float32
BF16 = jnp.bfloat16


def lane_iota(rows):
    return lax.broadcasted_iota(jnp.int32, (rows, LANES), 1)


def split(value):
    high = value.astype(BF16)
    return high, (value - high.astype(F32)).astype(BF16)


def kernel(
    press, gap, coupling, pattern, home,
    strip, gap_in, coup, pattern_in, rows_v, extra, extra_own, sendrows,
    gap_pad, c_right, c_left, c_down, e_coef, mix_hi, mix_lo, x_hi, x_lo, halo_out, halo_in,
    load_sem, in_send, in_recv, z_send, z_recv, out_send, out_recv, own_sem,
):
    space = lax.axis_index("space")
    mode = lax.axis_index("modes")
    count = lax.axis_size("space")
    y_lo = lax.rem(lax.div(space, ZRUN), 2)

    def swapped(index, bit):
        return index + bit * (lax.rem(index, 2) * 2 + lax.div(index, 2) - index)

    quarter = swapped(mode, y_lo)
    hi, core = lax.div(mode, 2), lax.rem(mode, 2)
    group = [(1 - hi) * 2 + core, (1 - hi) * 2 + 1 - core, hi * 2 + 1 - core]
    group_quarter = [swapped(peer, y_lo) for peer in group]

    def beside(step):
        other = lax.rem(space + step + count, count)
        other_y = lax.rem(lax.div(other, ZRUN), 2)
        return (other, swapped(quarter, other_y))

    before, after = beside(-1), beside(1)

    def columns(t):
        return slice(t * LANES, (t + 1) * LANES)

    press_loads = [pltpu.make_async_copy(press.at[:, columns(t)], strip.at[t], load_sem.at[t]) for t in range(4)]
    gap_loads = [pltpu.make_async_copy(gap.at[:, columns(t)], gap_in.at[t], load_sem.at[4 + t]) for t in range(4)]
    coup_load = pltpu.make_async_copy(coupling, coup, load_sem.at[8])
    pattern_load = pltpu.make_async_copy(pattern, pattern_in, load_sem.at[9])
    for load in press_loads + gap_loads + [coup_load, pattern_load]:
        load.start()

    barrier = pltpu.get_barrier_semaphore()
    for peer in group:
        pl.semaphore_signal(barrier, inc=1, device_id=(space, peer), device_id_type=MESH)
    for peer in (before, after):
        pl.semaphore_signal(barrier, inc=1, device_id=peer, device_id_type=MESH)

    for load in press_loads:
        load.wait()

    def own_rows(g, carry):
        at = pl.ds(pl.multiple_of(g * 8, 8), 8)
        lane = lane_iota(8)
        parts = [jnp.zeros((8, LANES), F32) for _ in range(4)]
        for r in range(ROWS):
            start = 6 * (r + 2)
            inside = (lane >= start) & (lane < start + 4)
            for t in range(4):
                value = strip[t, pl.ds(g * (8 * ROWS) + r, 8, stride=ROWS), :]
                sendrows[t, r, at, :] = value
                parts[t] = jnp.where(inside, pltpu.roll(value, start + 2, 1), parts[t])
        nothing = jnp.zeros((8, LANES), F32)
        place = lax.rem(lane, 6)
        moved = [pltpu.roll(part, 2, 1) for part in parts] + [nothing]
        for t in range(4):
            left = parts[t - 1] if t else nothing
            value = jnp.where(place < 2, left, jnp.where(place == 2, parts[t], moved[t]))
            extra_own[t, at, :] = jnp.where(place < 4, value, moved[t + 1])
        return carry

    lax.fori_loop(0, BLOCK // 8, own_rows, 0)

    pl.semaphore_wait(barrier, 5)

    mine = pl.multiple_of(mode * BLOCK, BLOCK)

    def row_copy(peer, peer_quarter, row, rows, slot, source):
        return pltpu.make_async_remote_copy(
            src_ref=sendrows.at[peer_quarter, pl.ds(row, rows)],
            dst_ref=rows_v.at[pl.ds(row + 2, rows), pl.ds(pl.multiple_of(source * BLOCK, BLOCK), BLOCK)],
            send_sem=in_send.at[slot, peer],
            recv_sem=in_recv.at[slot, source],
            device_id=(space, peer),
            device_id_type=MESH,
        )

    def extra_copy(peer, peer_quarter, source):
        return pltpu.make_async_remote_copy(
            src_ref=extra_own.at[peer_quarter],
            dst_ref=extra.at[0, pl.ds(pl.multiple_of(source * BLOCK, BLOCK), BLOCK)],
            send_sem=in_send.at[CHUNKS + 2, peer],
            recv_sem=in_recv.at[CHUNKS + 2, source],
            device_id=(space, peer),
            device_id_type=MESH,
        )

    for row, slot in ((0, CHUNKS), (14, CHUNKS + 1)):
        for peer, peer_quarter in zip(group, group_quarter):
            row_copy(peer, peer_quarter, row, 2, slot, mode).start()
    for peer, peer_quarter in zip(group, group_quarter):
        extra_copy(peer, peer_quarter, mode).start()
    for c in range(CHUNKS):
        for peer, peer_quarter in zip(group, group_quarter):
            row_copy(peer, peer_quarter, 2 * c + 2, 2, c, mode).start()

    for load in gap_loads:
        load.wait()
    for r in range(ROWS):
        slabs = [gap_in[t, pl.ds(r, K, stride=ROWS), :] for t in range(4)]
        slabs = [jnp.broadcast_to(slabs[0][:, :1], (K, LANES)), *slabs, jnp.broadcast_to(slabs[3][:, LANES - 1 :], (K, LANES))]
        for t in range(6):
            gap_pad[r + 2, :, columns(t)] = slabs[t]

    def z_copy(source, target, slot, device):
        return pltpu.make_async_remote_copy(
            src_ref=source, dst_ref=target, send_sem=z_send.at[slot], recv_sem=z_recv.at[slot],
            device_id=device, device_id_type=MESH,
        )

    gap_copies = [
        z_copy(gap_pad.at[pl.ds(2, 2)], gap_pad.at[pl.ds(ROWS + 2, 2)], 0, before),
        z_copy(gap_pad.at[pl.ds(ROWS, 2)], gap_pad.at[pl.ds(0, 2)], 1, after),
    ]
    for copy in gap_copies:
        copy.start()

    extra[0, pl.ds(mine, BLOCK), :] = extra_own[quarter]
    for r in range(ROWS):
        rows_v[r + 2, pl.ds(mine, BLOCK), :] = sendrows[quarter, r]

    coup_load.wait()
    pattern_load.wait()
    wide = lax.broadcasted_iota(jnp.int32, (1, MODES), 1)
    for k in range(K):
        for b in range(4):
            scale = [pattern_in[b, c : c + 1, k : k + 1].astype(F32) for c in range(4)]
            factor = jnp.where(
                wide < 128,
                jnp.where(wide < 64, scale[0], scale[1]),
                jnp.where(wide < 192, scale[2], scale[3]),
            )
            high, low = split(coup[k, b * BLOCK : (b + 1) * BLOCK, :] * factor)
            mix_hi[b * BLOCK : (b + 1) * BLOCK, k * MODES : (k + 1) * MODES] = high
            mix_lo[b * BLOCK : (b + 1) * BLOCK, k * MODES : (k + 1) * MODES] = low

    for copy in gap_copies:
        copy.wait_recv()

    @pl.when(space == 0)
    def _():
        gap_pad[1] = gap_pad[2]

    @pl.when(space == count - 1)
    def _():
        gap_pad[ROWS + 2] = gap_pad[ROWS + 1]

    def tile(index, side):
        return gap_pad[index, :, pl.ds(pl.multiple_of((quarter + side) * LANES, LANES), LANES)]

    lane8 = lane_iota(8)

    def coefficients(index, slab):
        left, here, right = tile(index, 0), tile(index, 1), tile(index, 2)
        below = tile(jnp.minimum(index + 1, ROWS + 3), 1)
        next_cell = jnp.where(lane8 == LANES - 1, pltpu.roll(right, LANES - 1, 1), pltpu.roll(here, LANES - 1, 1))
        last_cell = jnp.where(lane8 == 0, pltpu.roll(left, 1, 1), pltpu.roll(here, 1, 1))
        for ref, value in ((c_right, next_cell), (c_left, last_cell), (c_down, below)):
            ref[index] = 0.5 * (here + value)
        edge_left = jnp.where(lane8 < 2, pltpu.roll(left, 2, 1), pltpu.roll(here, 2, 1))
        edge_right = jnp.where(lane8 < 2, pltpu.roll(here, 2, 1), pltpu.roll(right, 2, 1))
        both = jnp.where(lane8 < 3, edge_left, pltpu.roll(edge_right, 2, 1))
        start = 6 * index
        return jnp.where((lane8 >= start) & (lane8 < start + 6), pltpu.roll(both, start, 1), slab)

    slab = lax.fori_loop(0, ROWS + 4, coefficients, jnp.zeros((8, LANES), F32))
    for n, shift in enumerate((LANES - 1, 1, LANES - 6, 6)):
        e_coef[n] = 0.5 * (slab + pltpu.roll(slab, shift, 1))

    for slot, row in ((CHUNKS, 0), (CHUNKS + 1, 14)):
        for peer in group:
            row_copy(peer, 0, row, 2, slot, peer).wait_recv()
    for peer in group:
        extra_copy(peer, 0, peer).wait_recv()

    lane32 = lane_iota(32)
    for n, shift in enumerate((LANES - 12, 32)):
        packed = jnp.zeros((32, LANES), F32)
        for g in range(8):
            moved = pltpu.roll(extra[0, 32 * g : 32 * g + 32, :], (shift + 16 * g) % LANES, 1)
            packed = jnp.where((lane32 >= 16 * g) & (lane32 < 16 * g + 16), moved, packed)
        halo_out[n] = packed

    edge_copies = [
        z_copy(halo_out.at[0], halo_in.at[1], 2, before),
        z_copy(halo_out.at[1], halo_in.at[0], 3, after),
        z_copy(rows_v.at[pl.ds(2, 2)], rows_v.at[pl.ds(ROWS + 2, 2)], 4, before),
        z_copy(rows_v.at[pl.ds(ROWS, 2)], rows_v.at[pl.ds(0, 2)], 5, after),
    ]
    for copy in edge_copies:
        copy.start()

    top, bottom = space == 0, space == count - 1

    def put(k, g, column, value):
        high, low = split(value)
        at = pl.ds(pl.multiple_of(k * MODES + g * 16, 16), 16)
        x_hi[at, column : column + LANES] = high
        x_lo[at, column : column + LANES] = low

    column = lax.rem(lane8[:1], 6)
    outside = ((column == 1) & (quarter == 0)) | ((column == 4) & (quarter == 3))

    def extra_terms(g, carry):
        v = extra[0, pl.ds(pl.multiple_of(g * 16, 16), 16), :]
        diffs = [v - pltpu.roll(v, shift, 1) for shift in (LANES - 1, 1, LANES - 6, 6)]
        for k in range(K):
            total = e_coef[0, k : k + 1, :] * diffs[0]
            for n in range(1, 4):
                total = total + e_coef[n, k : k + 1, :] * diffs[n]
            put(k, g, 0, total)
        return carry

    def take_edges():
        for copy in edge_copies:
            copy.wait_recv()

        @pl.when(top)
        def _():
            rows_v[0:2] = jnp.zeros((2, MODES, LANES), F32)

        @pl.when(bottom)
        def _():
            rows_v[ROWS + 2 : ROWS + 4] = jnp.zeros((2, MODES, LANES), F32)

        upper = jnp.where(top, 0.0, halo_in[0])
        lower = jnp.where(bottom, 0.0, halo_in[1])
        for g in range(8):
            at = slice(32 * g, 32 * g + 32)
            value = jnp.where(lane32 < 12, pltpu.roll(upper, (LANES - 16 * g) % LANES, 1), extra[0, at, :])
            inside = (lane32 >= 108) & (lane32 < 120)
            extra[0, at, :] = jnp.where(inside, pltpu.roll(lower, (108 - 16 * g) % LANES, 1), value)

    lane16 = lane_iota(16)

    def terms(base, side_index, index):
        for g in range(GROUPS):
            at = slice(g * 16, g * 16 + 16)
            v = [rows_v[base + n, at, :] for n in range(4)]
            side = extra[side_index, at, :]
            down = [v[n] - v[n + 1] for n in range(3)]
            diffs = []
            for n in range(2):
                here = v[n + 1]
                lane = 6 * (index + n)
                left = jnp.where(lane16 == 0, pltpu.roll(side, LANES - 1 - lane, 1), pltpu.roll(here, 1, 1))
                right = jnp.where(
                    lane16 == LANES - 1, pltpu.roll(side, LANES - 5 - lane, 1), pltpu.roll(here, LANES - 1, 1)
                )
                diffs.append((here - left, here - right))
            for k in range(K):
                flux = [c_down[index - 1 + n, k : k + 1, :] * down[n] for n in range(3)]
                for n in range(2):
                    total = (
                        c_left[index + n, k : k + 1, :] * diffs[n][0]
                        + c_right[index + n, k : k + 1, :] * diffs[n][1]
                    )
                    put(k, g, n * LANES, total + (flux[n + 1] - flux[n]))

    def home_copy(peer, owner_of_block, pair, their_quarter):
        return pltpu.make_async_remote_copy(
            src_ref=rows_v.at[pl.ds(DAMPED + 2 * pair, 2), pl.ds(pl.multiple_of(owner_of_block * BLOCK, BLOCK), BLOCK)],
            dst_ref=home.at[their_quarter, pl.ds(2 * pair, 2)],
            send_sem=out_send.at[pair, peer],
            recv_sem=out_recv.at[pair, their_quarter],
            device_id=(space, peer),
            device_id_type=MESH,
        )

    last = ROWS // 2

    def own_copy(pair):
        return pltpu.make_async_copy(
            rows_v.at[pl.ds(DAMPED + 2 * pair, 2), pl.ds(mine, BLOCK)], home.at[quarter, pl.ds(2 * pair, 2)], own_sem.at[pair]
        )

    again = 2 * last - 2

    def task(n, carry):
        is_extra = (n == 0) | (n == again)
        m = n - jnp.where(n > again, 1, 0)
        is_first = (m == 1) | (lax.rem(m, 2) == 0)
        f = lax.rem(jnp.where(m == 1, 1, m // 2 + 1), last + 1)
        d = lax.rem(jnp.maximum(m - 1, 0) // 2, last)
        base = jnp.where(is_first, 2 * f, FIRST + 2 * d)
        target = jnp.where(is_first, FIRST + 2 * f, DAMPED + 2 * d)
        target = jnp.where(is_extra, DAMPED + ROWS, target)
        index = jnp.where(is_first, 2 * f + 1, 2 * d + 2)

        @pl.when(jnp.logical_not(is_extra) & is_first & (f >= 1) & (f <= CHUNKS))
        def _():
            for peer in group:
                row_copy(peer, 0, 2 * f, 2, f - 1, peer).wait_recv()

        @pl.when(n == again)
        def _():
            take_edges()

        @pl.when(is_extra)
        def _():
            lax.fori_loop(0, GROUPS, extra_terms, 0)

        @pl.when(jnp.logical_not(is_extra))
        def _():
            terms(base, jnp.where(is_first, 0, 1), index)

        result = (
            jnp.dot(mix_hi[...], x_hi[...], preferred_element_type=F32)
            + jnp.dot(mix_hi[...], x_lo[...], preferred_element_type=F32)
            + jnp.dot(mix_lo[...], x_hi[...], preferred_element_type=F32)
        )
        rows_v[target] = jnp.where(is_first & (f == 0) & top, 0.0, result[:, :LANES])
        rows_v[target + 1] = jnp.where(is_first & (f == last) & bottom, 0.0, result[:, LANES:])

        @pl.when(is_extra)
        def _():
            extra[1] = jnp.where(outside, 0.0, rows_v[DAMPED + ROWS])

        @pl.when(jnp.logical_not(is_extra | is_first))
        def _():
            for peer in group:
                home_copy(peer, peer, d, quarter).start()
            own_copy(d).start()

        return carry

    lax.fori_loop(0, 2 * last + 3, task, 0)

    for pair in range(last):
        for peer, peer_quarter in zip(group, group_quarter):
            home_copy(peer, mode, pair, peer_quarter).wait_recv()
        own_copy(pair).wait()

    for slot, row in [(c, 2 * c + 2) for c in range(CHUNKS)] + [(CHUNKS, 0), (CHUNKS + 1, 14)]:
        for peer in group:
            row_copy(peer, 0, row, 2, slot, mode).wait_send()
    for peer in group:
        extra_copy(peer, 0, mode).wait_send()
        for pair in range(ROWS // 2):
            home_copy(peer, peer, pair, quarter).wait_send()
    for copy in gap_copies + edge_copies:
        copy.wait_send()


def arrange(home, out, taken, laid, load_sem, store_sem):
    rows = ROWS // 2
    places = [(n, t) for n in range(2) for t in range(4)]
    stores = [
        pltpu.make_async_copy(laid.at[n, t], out.at[:, n, :, t * LANES : (t + 1) * LANES], store_sem.at[n, t])
        for n, t in places
    ]
    loads = [
        pltpu.make_async_copy(home.at[t, pl.ds(n * rows, rows)], taken.at[n, t], load_sem.at[n, t]) for n, t in places
    ]
    for load in loads:
        load.start()
    for load, store, (n, t) in zip(loads, stores, places):
        load.wait()
        flat = laid.at[n, t].reshape(BLOCK * rows, LANES)
        for r in range(rows):
            flat[pl.ds(r, BLOCK, stride=rows), :] = taken[n, t, r]
        store.start()
    for store in stores:
        store.wait()


def per_device(pressure, gap_terms, coupling, pattern):
    cells = pressure.shape[2]
    vmem = pltpu.VMEM
    result = pl.pallas_call(
        kernel,
        out_shape=jax.ShapeDtypeStruct((4, ROWS, BLOCK, LANES), F32),
        in_specs=[
            pl.BlockSpec(memory_space=pl.ANY),
            pl.BlockSpec(memory_space=pl.ANY),
            pl.BlockSpec(memory_space=pl.ANY),
            pl.BlockSpec(memory_space=pl.ANY),
        ],
        out_specs=pl.BlockSpec(memory_space=pl.ANY),
        scratch_shapes=[
            vmem((4, BLOCK * ROWS, LANES), F32),
            vmem((4, K * ROWS, LANES), F32),
            vmem((K, MODES, MODES), F32),
            vmem((4, 4, K), jnp.int32),
            vmem((DAMPED + ROWS + 2, MODES, LANES), F32),
            vmem((2, MODES, LANES), F32),
            vmem((4, BLOCK, LANES), F32),
            vmem((4, ROWS, BLOCK, LANES), F32),
            vmem((ROWS + 4, K, cells + 2 * LANES), F32),
            vmem((ROWS + 4, K, LANES), F32),
            vmem((ROWS + 4, K, LANES), F32),
            vmem((ROWS + 4, K, LANES), F32),
            vmem((4, K, LANES), F32),
            vmem((MODES, K * MODES), BF16),
            vmem((MODES, K * MODES), BF16),
            vmem((K * MODES, 2 * LANES), BF16),
            vmem((K * MODES, 2 * LANES), BF16),
            vmem((2, 32, LANES), F32),
            vmem((2, 32, LANES), F32),
            pltpu.SemaphoreType.DMA((10,)),
            pltpu.SemaphoreType.DMA((CHUNKS + 3, 4)),
            pltpu.SemaphoreType.DMA((CHUNKS + 3, 4)),
            pltpu.SemaphoreType.DMA((6,)),
            pltpu.SemaphoreType.DMA((6,)),
            pltpu.SemaphoreType.DMA((ROWS // 2, 4)),
            pltpu.SemaphoreType.DMA((ROWS // 2, 4)),
            pltpu.SemaphoreType.DMA((ROWS // 2,)),
        ],
        compiler_params=pltpu.CompilerParams(
            collective_id=0, has_side_effects=True, vmem_limit_bytes=56 * 1024 * 1024
        ),
        cost_estimate=pl.CostEstimate(flops=26_000_000_000, bytes_accessed=7_000_000, transcendentals=0),
        name="galerkin_twice",
    )(pressure.reshape(BLOCK * ROWS, cells), gap_terms.reshape(K * ROWS, cells), coupling, pattern.transpose(1, 2, 0))
    out = pl.pallas_call(
        arrange,
        out_shape=jax.ShapeDtypeStruct((BLOCK, 2, ROWS // 2, cells), F32),
        in_specs=[pl.BlockSpec(memory_space=pl.ANY)],
        out_specs=pl.BlockSpec(memory_space=pl.ANY),
        scratch_shapes=[
            vmem((2, 4, ROWS // 2, BLOCK, LANES), F32),
            vmem((2, 4, BLOCK, ROWS // 2, LANES), F32),
            pltpu.SemaphoreType.DMA((2, 4)),
            pltpu.SemaphoreType.DMA((2, 4)),
        ],
        compiler_params=pltpu.CompilerParams(vmem_limit_bytes=60 * 1024 * 1024),
        cost_estimate=pl.CostEstimate(flops=0, bytes_accessed=4_200_000, transcendentals=0),
        name="arrange",
    )(result)
    return out.reshape(pressure.shape)


def solution(mesh):
    placed = (P("modes", "space", None), P(None, "space", None), P(), P())
    return jax.shard_map(
        per_device, mesh=mesh, in_specs=placed, out_specs=P("modes", "space", None), check_vma=False
    )
```

```python
import functools

import jax
import jax.numpy as jnp
from jax import lax
from jax.experimental import pallas as pl
from jax.experimental.pallas import tpu as pltpu
from jax.sharding import PartitionSpec as P

MESH = pl.DeviceIdType.MESH
K = 8
MODES = 256
BLOCK = 64
ROWS = 16
LANES = 128
ZRUN = 8
GROUPS = MODES // 16
CHUNKS = 6
GATE = 3
MEET = 1
FIRST = ROWS + 4
DAMPED = 2 * ROWS + 6
F32 = jnp.float32
BF16 = jnp.bfloat16


def lane_iota(rows):
    return lax.broadcasted_iota(jnp.int32, (rows, LANES), 1)


def split(value):
    high = value.astype(BF16)
    return high, (value - high.astype(F32)).astype(BF16)


def kernel(
    press, gap, coupling, pattern, home,
    strip, gap_in, coup, pattern_in, rows_v, extra, extra_own, sendrows,
    gap_pad, c_right, c_left, c_down, e_coef, mix_hi, mix_lo, x_hi, x_lo, halo_out, halo_in, gap_halo, gap_extra,
    load_sem, in_send, in_recv, z_send, z_recv, out_send, out_recv, own_sem, entered, beside_in, proceed,
):
    space = lax.axis_index("space")
    mode = lax.axis_index("modes")
    count = lax.axis_size("space")
    y_lo = lax.rem(lax.div(space, ZRUN), 2)

    def swapped(index, bit):
        return index + bit * (lax.rem(index, 2) * 2 + lax.div(index, 2) - index)

    quarter = swapped(mode, y_lo)
    hi, core = lax.div(mode, 2), lax.rem(mode, 2)
    group = [(1 - hi) * 2 + core, (1 - hi) * 2 + 1 - core, hi * 2 + 1 - core]
    group_quarter = [swapped(peer, y_lo) for peer in group]

    def beside(step):
        other = lax.rem(space + step + count, count)
        other_y = lax.rem(lax.div(other, ZRUN), 2)
        return (other, swapped(quarter, other_y))

    before, after = beside(-1), beside(1)

    def columns(t):
        return slice(t * LANES, (t + 1) * LANES)

    press_loads = [pltpu.make_async_copy(press.at[:, columns(t)], strip.at[t], load_sem.at[t]) for t in range(4)]
    gap_loads = [pltpu.make_async_copy(gap.at[:, columns(t)], gap_in.at[t], load_sem.at[4 + t]) for t in range(4)]
    coup_load = pltpu.make_async_copy(coupling, coup, load_sem.at[8])
    pattern_load = pltpu.make_async_copy(pattern, pattern_in, load_sem.at[9])
    for load in press_loads + gap_loads + [coup_load, pattern_load]:
        load.start()

    is_gate = mode == GATE
    barrier = pltpu.get_barrier_semaphore()
    for peer in group:

        @pl.when(peer != GATE)
        def _():
            pl.semaphore_signal(barrier, inc=1, device_id=(space, peer), device_id_type=MESH)

    @pl.when(is_gate)
    def _():
        for peer in (before, after):
            pl.semaphore_signal(barrier, inc=1, device_id=peer, device_id_type=MESH)

    for load in press_loads:
        load.wait()

    def own_rows(g, carry):
        at = pl.ds(pl.multiple_of(g * 8, 8), 8)
        lane = lane_iota(8)
        parts = [jnp.zeros((8, LANES), F32) for _ in range(4)]
        for r in range(ROWS):
            start = 6 * (r + 2)
            inside = (lane >= start) & (lane < start + 4)
            for t in range(4):
                value = strip[t, pl.ds(g * (8 * ROWS) + r, 8, stride=ROWS), :]
                sendrows[t, r, at, :] = value
                parts[t] = jnp.where(inside, pltpu.roll(value, start + 2, 1), parts[t])
        nothing = jnp.zeros((8, LANES), F32)
        place = lax.rem(lane, 6)
        moved = [pltpu.roll(part, 2, 1) for part in parts] + [nothing]
        for t in range(4):
            left = parts[t - 1] if t else nothing
            value = jnp.where(place < 2, left, jnp.where(place == 2, parts[t], moved[t]))
            extra_own[t, at, :] = jnp.where(place < 4, value, moved[t + 1])
        return carry

    lax.fori_loop(0, BLOCK // 8, own_rows, 0)

    @pl.when(jnp.logical_not(is_gate))
    def _():
        pl.semaphore_wait(barrier, 3)
        pl.semaphore_signal(entered, inc=1, device_id=(space, GATE), device_id_type=MESH)

    @pl.when(is_gate)
    def _():
        pl.semaphore_wait(entered, 3)

    def meet_neighbours():
        pl.semaphore_wait(barrier, 2)
        for peer in (before, after):
            pl.semaphore_signal(beside_in, inc=1, device_id=peer, device_id_type=MESH)

    def pass_on():
        pl.semaphore_wait(beside_in, 2)
        for peer in group:
            pl.semaphore_signal(proceed, inc=1, device_id=(space, peer), device_id_type=MESH)

    mine = pl.multiple_of(mode * BLOCK, BLOCK)

    def row_copy(peer, peer_quarter, row, rows, slot, source):
        return pltpu.make_async_remote_copy(
            src_ref=sendrows.at[peer_quarter, pl.ds(row, rows)],
            dst_ref=rows_v.at[pl.ds(row + 2, rows), pl.ds(pl.multiple_of(source * BLOCK, BLOCK), BLOCK)],
            send_sem=in_send.at[slot, peer],
            recv_sem=in_recv.at[slot, source],
            device_id=(space, peer),
            device_id_type=MESH,
        )

    def extra_copy(peer, peer_quarter, source):
        return pltpu.make_async_remote_copy(
            src_ref=extra_own.at[peer_quarter],
            dst_ref=extra.at[0, pl.ds(pl.multiple_of(source * BLOCK, BLOCK), BLOCK)],
            send_sem=in_send.at[CHUNKS + 2, peer],
            recv_sem=in_recv.at[CHUNKS + 2, source],
            device_id=(space, peer),
            device_id_type=MESH,
        )

    for peer, peer_quarter in zip(group, group_quarter):
        extra_copy(peer, peer_quarter, mode).start()
    for row in (0, 2, 14, 4, 6, 8, 10, 12):
        slot = {0: CHUNKS, 14: CHUNKS + 1}.get(row, row // 2 - 1)
        for peer, peer_quarter in zip(group, group_quarter):
            row_copy(peer, peer_quarter, row, 2, slot, mode).start()

    for load in gap_loads:
        load.wait()
    for r in range(ROWS):
        slabs = [gap_in[t, pl.ds(r, K, stride=ROWS), :] for t in range(4)]
        slabs = [jnp.broadcast_to(slabs[0][:, :1], (K, LANES)), *slabs, jnp.broadcast_to(slabs[3][:, LANES - 1 :], (K, LANES))]
        for t in range(6):
            for place in {0: (0, 1, 2), ROWS - 1: (ROWS + 1, ROWS + 2, ROWS + 3)}.get(r, (r + 2,)):
                gap_pad[place, :, columns(t)] = slabs[t]

    def z_copy(source, target, slot, device):
        return pltpu.make_async_remote_copy(
            src_ref=source, dst_ref=target, send_sem=z_send.at[slot], recv_sem=z_recv.at[slot],
            device_id=device, device_id_type=MESH,
        )

    gap_copies = [
        z_copy(gap_pad.at[pl.ds(2, 2)], gap_halo.at[1], 0, before),
        z_copy(gap_pad.at[pl.ds(ROWS, 2)], gap_halo.at[0], 1, after),
    ]

    extra[0, pl.ds(mine, BLOCK), :] = extra_own[quarter]
    for r in range(ROWS):
        rows_v[r + 2, pl.ds(mine, BLOCK), :] = sendrows[quarter, r]

    coup_load.wait()
    pattern_load.wait()
    wide = lax.broadcasted_iota(jnp.int32, (1, MODES), 1)
    for k in range(K):
        for b in range(4):
            scale = [pattern_in[b, c : c + 1, k : k + 1].astype(F32) for c in range(4)]
            factor = jnp.where(
                wide < 128,
                jnp.where(wide < 64, scale[0], scale[1]),
                jnp.where(wide < 192, scale[2], scale[3]),
            )
            high, low = split(coup[k, b * BLOCK : (b + 1) * BLOCK, :] * factor)
            mix_hi[b * BLOCK : (b + 1) * BLOCK, k * MODES : (k + 1) * MODES] = high
            mix_lo[b * BLOCK : (b + 1) * BLOCK, k * MODES : (k + 1) * MODES] = low

    def tile(index, side):
        return gap_pad[index, :, pl.ds(pl.multiple_of((quarter + side) * LANES, LANES), LANES)]

    lane8 = lane_iota(8)

    def coefficients(step, carry, skip):
        index = step + jnp.where(step >= 2, skip, 0)
        left, here, right = tile(index, 0), tile(index, 1), tile(index, 2)
        below = tile(jnp.minimum(index + 1, ROWS + 3), 1)
        next_cell = jnp.where(lane8 == LANES - 1, pltpu.roll(right, LANES - 1, 1), pltpu.roll(here, LANES - 1, 1))
        last_cell = jnp.where(lane8 == 0, pltpu.roll(left, 1, 1), pltpu.roll(here, 1, 1))
        for ref, value in ((c_right, next_cell), (c_left, last_cell), (c_down, below)):
            ref[index] = 0.5 * (here + value)
        edge_left = jnp.where(lane8 < 2, pltpu.roll(left, 2, 1), pltpu.roll(here, 2, 1))
        edge_right = jnp.where(lane8 < 2, pltpu.roll(here, 2, 1), pltpu.roll(right, 2, 1))
        both = jnp.where(lane8 < 3, edge_left, pltpu.roll(edge_right, 2, 1))
        start = 6 * index
        inside = (lane8 >= start) & (lane8 < start + 6)
        gap_extra[...] = jnp.where(inside, pltpu.roll(both, start, 1), gap_extra[...])
        return carry

    def tables(steps, skip):
        lax.fori_loop(0, steps, functools.partial(coefficients, skip=skip), 0)
        slab = gap_extra[...]
        for n, shift in enumerate((LANES - 1, 1, LANES - 6, 6)):
            e_coef[n] = 0.5 * (slab + pltpu.roll(slab, shift, 1))

    gap_extra[...] = jnp.zeros((K, LANES), F32)
    tables(ROWS + 4, 0)

    for peer in group:
        extra_copy(peer, 0, peer).wait_recv()
        row_copy(peer, 0, 0, 2, CHUNKS, peer).wait_recv()

    lane32 = lane_iota(32)
    for n, shift in enumerate((LANES - 12, 32)):
        packed = jnp.zeros((32, LANES), F32)
        for g in range(8):
            moved = pltpu.roll(extra[0, 32 * g : 32 * g + 32, :], (shift + 16 * g) % LANES, 1)
            packed = jnp.where((lane32 >= 16 * g) & (lane32 < 16 * g + 16), moved, packed)
        halo_out[n] = packed

    edge_copies = [
        z_copy(halo_out.at[0], halo_in.at[1], 2, before),
        z_copy(halo_out.at[1], halo_in.at[0], 3, after),
        z_copy(rows_v.at[pl.ds(2, 2)], rows_v.at[pl.ds(ROWS + 2, 2)], 4, before),
        z_copy(rows_v.at[pl.ds(ROWS, 2)], rows_v.at[pl.ds(0, 2)], 5, after),
    ]

    def send_edges():
        for peer in group:
            row_copy(peer, 0, 14, 2, CHUNKS + 1, peer).wait_recv()
        for copy in gap_copies + edge_copies:
            copy.start()

    top, bottom = space == 0, space == count - 1

    def put(k, g, column, value):
        high, low = split(value)
        at = pl.ds(pl.multiple_of(k * MODES + g * 16, 16), 16)
        x_hi[at, column : column + LANES] = high
        x_lo[at, column : column + LANES] = low

    column = lax.rem(lane8[:1], 6)
    outside = ((column == 1) & (quarter == 0)) | ((column == 4) & (quarter == 3))

    def extra_terms(g, carry):
        v = extra[0, pl.ds(pl.multiple_of(g * 16, 16), 16), :]
        diffs = [v - pltpu.roll(v, shift, 1) for shift in (LANES - 1, 1, LANES - 6, 6)]
        for k in range(K):
            total = e_coef[0, k : k + 1, :] * diffs[0]
            for n in range(1, 4):
                total = total + e_coef[n, k : k + 1, :] * diffs[n]
            put(k, g, 0, total)
        return carry

    def take_edges():
        for copy in gap_copies + edge_copies:
            copy.wait_recv()

        @pl.when(jnp.logical_not(top))
        def _():
            gap_pad[0:2] = gap_halo[0]

        @pl.when(jnp.logical_not(bottom))
        def _():
            gap_pad[ROWS + 2 : ROWS + 4] = gap_halo[1]

        tables(5, ROWS - 1)

        @pl.when(top)
        def _():
            rows_v[0:2] = jnp.zeros((2, MODES, LANES), F32)

        @pl.when(bottom)
        def _():
            rows_v[ROWS + 2 : ROWS + 4] = jnp.zeros((2, MODES, LANES), F32)

        upper = jnp.where(top, 0.0, halo_in[0])
        lower = jnp.where(bottom, 0.0, halo_in[1])
        for g in range(8):
            at = slice(32 * g, 32 * g + 32)
            value = jnp.where(lane32 < 12, pltpu.roll(upper, (LANES - 16 * g) % LANES, 1), extra[0, at, :])
            inside = (lane32 >= 108) & (lane32 < 120)
            extra[0, at, :] = jnp.where(inside, pltpu.roll(lower, (108 - 16 * g) % LANES, 1), value)

    lane16 = lane_iota(16)

    def terms(base, side_index, index):
        for g in range(GROUPS):
            at = slice(g * 16, g * 16 + 16)
            v = [rows_v[base + n, at, :] for n in range(4)]
            side = extra[side_index, at, :]
            down = [v[n] - v[n + 1] for n in range(3)]
            diffs = []
            for n in range(2):
                here = v[n + 1]
                lane = 6 * (index + n)
                left = jnp.where(lane16 == 0, pltpu.roll(side, LANES - 1 - lane, 1), pltpu.roll(here, 1, 1))
                right = jnp.where(
                    lane16 == LANES - 1, pltpu.roll(side, LANES - 5 - lane, 1), pltpu.roll(here, LANES - 1, 1)
                )
                diffs.append((here - left, here - right))
            for k in range(K):
                flux = [c_down[index - 1 + n, k : k + 1, :] * down[n] for n in range(3)]
                for n in range(2):
                    total = (
                        c_left[index + n, k : k + 1, :] * diffs[n][0]
                        + c_right[index + n, k : k + 1, :] * diffs[n][1]
                    )
                    put(k, g, n * LANES, total + (flux[n + 1] - flux[n]))

    def home_copy(peer, owner_of_block, pair, their_quarter):
        return pltpu.make_async_remote_copy(
            src_ref=rows_v.at[pl.ds(DAMPED + 2 * pair, 2), pl.ds(pl.multiple_of(owner_of_block * BLOCK, BLOCK), BLOCK)],
            dst_ref=home.at[their_quarter, pl.ds(2 * pair, 2)],
            send_sem=out_send.at[pair, peer],
            recv_sem=out_recv.at[pair, their_quarter],
            device_id=(space, peer),
            device_id_type=MESH,
        )

    last = ROWS // 2

    def own_copy(pair):
        return pltpu.make_async_copy(
            rows_v.at[pl.ds(DAMPED + 2 * pair, 2), pl.ds(mine, BLOCK)], home.at[quarter, pl.ds(2 * pair, 2)], own_sem.at[pair]
        )

    again = 2 * last - 2

    def task(n, carry):
        is_extra = (n == 0) | (n == again)
        m = n - jnp.where(n > again, 1, 0)
        is_first = (m == 1) | (lax.rem(m, 2) == 0)
        f = lax.rem(jnp.where(m == 1, 1, m // 2 + 1), last + 1)
        d = lax.rem(jnp.maximum(m - 1, 0) // 2, last)
        base = jnp.where(is_first, 2 * f, FIRST + 2 * d)
        target = jnp.where(is_first, FIRST + 2 * f, DAMPED + 2 * d)
        target = jnp.where(is_extra, DAMPED + ROWS, target)
        index = jnp.where(is_first, 2 * f + 1, 2 * d + 2)

        @pl.when(jnp.logical_not(is_extra) & is_first & (f >= 1) & (f <= CHUNKS))
        def _():
            for peer in group:
                row_copy(peer, 0, 2 * f, 2, f - 1, peer).wait_recv()

        @pl.when((n == MEET) & is_gate)
        def _():
            meet_neighbours()

        @pl.when((n == MEET + 1) & is_gate)
        def _():
            pass_on()

        @pl.when((n == MEET + 2) & jnp.logical_not(is_gate))
        def _():
            pl.semaphore_wait(proceed, 1)

        @pl.when(n == MEET + 2)
        def _():
            send_edges()

        @pl.when(n == again)
        def _():
            take_edges()

        @pl.when(is_extra)
        def _():
            lax.fori_loop(0, GROUPS, extra_terms, 0)

        @pl.when(jnp.logical_not(is_extra))
        def _():
            terms(base, jnp.where(is_first, 0, 1), index)

        result = (
            jnp.dot(mix_hi[...], x_hi[...], preferred_element_type=F32)
            + jnp.dot(mix_hi[...], x_lo[...], preferred_element_type=F32)
            + jnp.dot(mix_lo[...], x_hi[...], preferred_element_type=F32)
        )
        rows_v[target] = jnp.where(is_first & (f == 0) & top, 0.0, result[:, :LANES])
        rows_v[target + 1] = jnp.where(is_first & (f == last) & bottom, 0.0, result[:, LANES:])

        @pl.when(is_extra)
        def _():
            extra[1] = jnp.where(outside, 0.0, rows_v[DAMPED + ROWS])

        @pl.when(jnp.logical_not(is_extra | is_first))
        def _():
            for peer in group:
                home_copy(peer, peer, d, quarter).start()
            own_copy(d).start()

        return carry

    lax.fori_loop(0, 2 * last + 3, task, 0)

    for pair in range(last):
        for peer, peer_quarter in zip(group, group_quarter):
            home_copy(peer, mode, pair, peer_quarter).wait_recv()
        own_copy(pair).wait()

    for slot, row in [(c, 2 * c + 2) for c in range(CHUNKS)] + [(CHUNKS, 0), (CHUNKS + 1, 14)]:
        for peer in group:
            row_copy(peer, 0, row, 2, slot, mode).wait_send()
    for peer in group:
        extra_copy(peer, 0, mode).wait_send()
        for pair in range(ROWS // 2):
            home_copy(peer, peer, pair, quarter).wait_send()
    for copy in gap_copies + edge_copies:
        copy.wait_send()


def arrange(home, out, taken, laid, load_sem, store_sem):
    rows = ROWS // 2
    places = [(n, t) for n in range(2) for t in range(4)]
    stores = [
        pltpu.make_async_copy(laid.at[n, t], out.at[:, n, :, t * LANES : (t + 1) * LANES], store_sem.at[n, t])
        for n, t in places
    ]
    loads = [
        pltpu.make_async_copy(home.at[t, pl.ds(n * rows, rows)], taken.at[n, t], load_sem.at[n, t]) for n, t in places
    ]
    for load in loads:
        load.start()
    for load, store, (n, t) in zip(loads, stores, places):
        load.wait()
        flat = laid.at[n, t].reshape(BLOCK * rows, LANES)
        for r in range(rows):
            flat[pl.ds(r, BLOCK, stride=rows), :] = taken[n, t, r]
        store.start()
    for store in stores:
        store.wait()


def per_device(pressure, gap_terms, coupling, pattern):
    cells = pressure.shape[2]
    vmem = pltpu.VMEM
    result = pl.pallas_call(
        kernel,
        out_shape=jax.ShapeDtypeStruct((4, ROWS, BLOCK, LANES), F32),
        in_specs=[
            pl.BlockSpec(memory_space=pl.ANY),
            pl.BlockSpec(memory_space=pl.ANY),
            pl.BlockSpec(memory_space=pl.ANY),
            pl.BlockSpec(memory_space=pl.ANY),
        ],
        out_specs=pl.BlockSpec(memory_space=pl.ANY),
        scratch_shapes=[
            vmem((4, BLOCK * ROWS, LANES), F32),
            vmem((4, K * ROWS, LANES), F32),
            vmem((K, MODES, MODES), F32),
            vmem((4, 4, K), jnp.int32),
            vmem((DAMPED + ROWS + 2, MODES, LANES), F32),
            vmem((2, MODES, LANES), F32),
            vmem((4, BLOCK, LANES), F32),
            vmem((4, ROWS, BLOCK, LANES), F32),
            vmem((ROWS + 4, K, cells + 2 * LANES), F32),
            vmem((ROWS + 4, K, LANES), F32),
            vmem((ROWS + 4, K, LANES), F32),
            vmem((ROWS + 4, K, LANES), F32),
            vmem((4, K, LANES), F32),
            vmem((MODES, K * MODES), BF16),
            vmem((MODES, K * MODES), BF16),
            vmem((K * MODES, 2 * LANES), BF16),
            vmem((K * MODES, 2 * LANES), BF16),
            vmem((2, 32, LANES), F32),
            vmem((2, 32, LANES), F32),
            vmem((2, 2, K, cells + 2 * LANES), F32),
            vmem((K, LANES), F32),
            pltpu.SemaphoreType.DMA((10,)),
            pltpu.SemaphoreType.DMA((CHUNKS + 3, 4)),
            pltpu.SemaphoreType.DMA((CHUNKS + 3, 4)),
            pltpu.SemaphoreType.DMA((6,)),
            pltpu.SemaphoreType.DMA((6,)),
            pltpu.SemaphoreType.DMA((ROWS // 2, 4)),
            pltpu.SemaphoreType.DMA((ROWS // 2, 4)),
            pltpu.SemaphoreType.DMA((ROWS // 2,)),
            pltpu.SemaphoreType.REGULAR,
            pltpu.SemaphoreType.REGULAR,
            pltpu.SemaphoreType.REGULAR,
        ],
        compiler_params=pltpu.CompilerParams(
            collective_id=0, has_side_effects=True, vmem_limit_bytes=56 * 1024 * 1024
        ),
        cost_estimate=pl.CostEstimate(flops=26_000_000_000, bytes_accessed=7_000_000, transcendentals=0),
        name="galerkin_twice",
    )(pressure.reshape(BLOCK * ROWS, cells), gap_terms.reshape(K * ROWS, cells), coupling, pattern.transpose(1, 2, 0))
    out = pl.pallas_call(
        arrange,
        out_shape=jax.ShapeDtypeStruct((BLOCK, 2, ROWS // 2, cells), F32),
        in_specs=[pl.BlockSpec(memory_space=pl.ANY)],
        out_specs=pl.BlockSpec(memory_space=pl.ANY),
        scratch_shapes=[
            vmem((2, 4, ROWS // 2, BLOCK, LANES), F32),
            vmem((2, 4, BLOCK, ROWS // 2, LANES), F32),
            pltpu.SemaphoreType.DMA((2, 4)),
            pltpu.SemaphoreType.DMA((2, 4)),
        ],
        compiler_params=pltpu.CompilerParams(vmem_limit_bytes=60 * 1024 * 1024),
        cost_estimate=pl.CostEstimate(flops=0, bytes_accessed=4_200_000, transcendentals=0),
        name="arrange",
    )(result)
    return out.reshape(pressure.shape)


def solution(mesh):
    placed = (P("modes", "space", None), P(None, "space", None), P(), P())
    return jax.shard_map(
        per_device, mesh=mesh, in_specs=placed, out_specs=P("modes", "space", None), check_vma=False
    )
```

```python
import functools

import jax
import jax.numpy as jnp
from jax import lax
from jax.experimental import pallas as pl
from jax.experimental.pallas import tpu as pltpu
from jax.sharding import PartitionSpec as P

MESH = pl.DeviceIdType.MESH
K = 8
MODES = 256
BLOCK = 64
ROWS = 16
LANES = 128
ZRUN = 8
GROUPS = MODES // 16
CHUNKS = 6
GATE = 3
MEET = 1
FIRST = ROWS + 4
DAMPED = 2 * ROWS + 6
F32 = jnp.float32
BF16 = jnp.bfloat16


def lane_iota(rows):
    return lax.broadcasted_iota(jnp.int32, (rows, LANES), 1)


def split(value):
    high = value.astype(BF16)
    return high, (value - high.astype(F32)).astype(BF16)


def kernel(
    press, gap, coupling, pattern, home,
    strip, gap_in, coup, pattern_in, rows_v, extra, extra_own, sendrows,
    gap_pad, c_right, c_left, c_down, e_coef, mix_hi, mix_lo, x_hi, x_lo, halo_out, halo_in, gap_halo, gap_extra,
    load_sem, in_send, in_recv, z_send, z_recv, out_send, out_recv, own_sem, entered, beside_in, proceed,
):
    space = lax.axis_index("space")
    mode = lax.axis_index("modes")
    count = lax.axis_size("space")
    y_lo = lax.rem(lax.div(space, ZRUN), 2)

    def swapped(index, bit):
        return index + bit * (lax.rem(index, 2) * 2 + lax.div(index, 2) - index)

    quarter = swapped(mode, y_lo)
    hi, core = lax.div(mode, 2), lax.rem(mode, 2)
    group = [(1 - hi) * 2 + core, (1 - hi) * 2 + 1 - core, hi * 2 + 1 - core]
    group_quarter = [swapped(peer, y_lo) for peer in group]

    def beside(step):
        other = lax.rem(space + step + count, count)
        other_y = lax.rem(lax.div(other, ZRUN), 2)
        return (other, swapped(quarter, other_y))

    before, after = beside(-1), beside(1)

    def columns(t):
        return slice(t * LANES, (t + 1) * LANES)

    press_loads = [pltpu.make_async_copy(press.at[:, columns(t)], strip.at[t], load_sem.at[t]) for t in range(4)]
    gap_loads = [pltpu.make_async_copy(gap.at[:, columns(t)], gap_in.at[t], load_sem.at[4 + t]) for t in range(4)]
    coup_load = pltpu.make_async_copy(coupling, coup, load_sem.at[8])
    pattern_load = pltpu.make_async_copy(pattern, pattern_in, load_sem.at[9])
    for load in press_loads + gap_loads + [coup_load, pattern_load]:
        load.start()

    is_gate = mode == GATE
    barrier = pltpu.get_barrier_semaphore()
    for peer in group:

        @pl.when(peer != GATE)
        def _():
            pl.semaphore_signal(barrier, inc=1, device_id=(space, peer), device_id_type=MESH)

    @pl.when(is_gate)
    def _():
        for peer in (before, after):
            pl.semaphore_signal(barrier, inc=1, device_id=peer, device_id_type=MESH)

    for load in press_loads:
        load.wait()

    def own_rows(g, carry):
        at = pl.ds(pl.multiple_of(g * 8, 8), 8)
        lane = lane_iota(8)
        parts = [jnp.zeros((8, LANES), F32) for _ in range(4)]
        for r in range(ROWS):
            start = 6 * (r + 2)
            inside = (lane >= start) & (lane < start + 4)
            for t in range(4):
                value = strip[t, pl.ds(g * (8 * ROWS) + r, 8, stride=ROWS), :]
                sendrows[t, r, at, :] = value
                parts[t] = jnp.where(inside, pltpu.roll(value, start + 2, 1), parts[t])
        nothing = jnp.zeros((8, LANES), F32)
        place = lax.rem(lane, 6)
        moved = [pltpu.roll(part, 2, 1) for part in parts] + [nothing]
        for t in range(4):
            left = parts[t - 1] if t else nothing
            value = jnp.where(place < 2, left, jnp.where(place == 2, parts[t], moved[t]))
            extra_own[t, at, :] = jnp.where(place < 4, value, moved[t + 1])
        return carry

    lax.fori_loop(0, BLOCK // 8, own_rows, 0)

    @pl.when(jnp.logical_not(is_gate))
    def _():
        pl.semaphore_wait(barrier, 3)
        pl.semaphore_signal(entered, inc=1, device_id=(space, GATE), device_id_type=MESH)

    @pl.when(is_gate)
    def _():
        pl.semaphore_wait(entered, 3)

    def meet_neighbours():
        pl.semaphore_wait(barrier, 2)
        for peer in (before, after):
            pl.semaphore_signal(beside_in, inc=1, device_id=peer, device_id_type=MESH)

    def pass_on():
        pl.semaphore_wait(beside_in, 2)
        for peer in group:
            pl.semaphore_signal(proceed, inc=1, device_id=(space, peer), device_id_type=MESH)

    mine = pl.multiple_of(mode * BLOCK, BLOCK)

    def row_copy(peer, peer_quarter, row, rows, slot, source):
        return pltpu.make_async_remote_copy(
            src_ref=sendrows.at[peer_quarter, pl.ds(row, rows)],
            dst_ref=rows_v.at[pl.ds(row + 2, rows), pl.ds(pl.multiple_of(source * BLOCK, BLOCK), BLOCK)],
            send_sem=in_send.at[slot, peer],
            recv_sem=in_recv.at[slot, source],
            device_id=(space, peer),
            device_id_type=MESH,
        )

    def extra_copy(peer, peer_quarter, source):
        return pltpu.make_async_remote_copy(
            src_ref=extra_own.at[peer_quarter],
            dst_ref=extra.at[0, pl.ds(pl.multiple_of(source * BLOCK, BLOCK), BLOCK)],
            send_sem=in_send.at[CHUNKS + 2, peer],
            recv_sem=in_recv.at[CHUNKS + 2, source],
            device_id=(space, peer),
            device_id_type=MESH,
        )

    for peer, peer_quarter in zip(group, group_quarter):
        extra_copy(peer, peer_quarter, mode).start()
    for row in (0, 2, 14, 4, 6, 8, 10, 12):
        slot = {0: CHUNKS, 14: CHUNKS + 1}.get(row, row // 2 - 1)
        for peer, peer_quarter in zip(group, group_quarter):
            row_copy(peer, peer_quarter, row, 2, slot, mode).start()

    for load in gap_loads:
        load.wait()
    for r in range(ROWS):
        slabs = [gap_in[t, pl.ds(r, K, stride=ROWS), :] for t in range(4)]
        slabs = [jnp.broadcast_to(slabs[0][:, :1], (K, LANES)), *slabs, jnp.broadcast_to(slabs[3][:, LANES - 1 :], (K, LANES))]
        for t in range(6):
            for place in {0: (0, 1, 2), ROWS - 1: (ROWS + 1, ROWS + 2, ROWS + 3)}.get(r, (r + 2,)):
                gap_pad[place, :, columns(t)] = slabs[t]

    def z_copy(source, target, slot, device):
        return pltpu.make_async_remote_copy(
            src_ref=source, dst_ref=target, send_sem=z_send.at[slot], recv_sem=z_recv.at[slot],
            device_id=device, device_id_type=MESH,
        )

    gap_copies = [
        z_copy(gap_pad.at[pl.ds(2, 2)], gap_halo.at[1], 0, before),
        z_copy(gap_pad.at[pl.ds(ROWS, 2)], gap_halo.at[0], 1, after),
    ]

    extra[0, pl.ds(mine, BLOCK), :] = extra_own[quarter]
    for r in range(ROWS):
        rows_v[r + 2, pl.ds(mine, BLOCK), :] = sendrows[quarter, r]

    coup_load.wait()
    pattern_load.wait()
    wide = lax.broadcasted_iota(jnp.int32, (1, MODES), 1)
    for k in range(K):
        for b in range(4):
            scale = [pattern_in[b, c : c + 1, k : k + 1].astype(F32) for c in range(4)]
            factor = jnp.where(
                wide < 128,
                jnp.where(wide < 64, scale[0], scale[1]),
                jnp.where(wide < 192, scale[2], scale[3]),
            )
            high, low = split(coup[k, b * BLOCK : (b + 1) * BLOCK, :] * factor)
            mix_hi[b * BLOCK : (b + 1) * BLOCK, k * MODES : (k + 1) * MODES] = high
            mix_lo[b * BLOCK : (b + 1) * BLOCK, k * MODES : (k + 1) * MODES] = low

    def tile(index, side):
        return gap_pad[index, :, pl.ds(pl.multiple_of((quarter + side) * LANES, LANES), LANES)]

    lane8 = lane_iota(8)

    def coefficients(step, carry, skip):
        index = step + jnp.where(step >= 2, skip, 0)
        left, here, right = tile(index, 0), tile(index, 1), tile(index, 2)
        below = tile(jnp.minimum(index + 1, ROWS + 3), 1)
        next_cell = jnp.where(lane8 == LANES - 1, pltpu.roll(right, LANES - 1, 1), pltpu.roll(here, LANES - 1, 1))
        last_cell = jnp.where(lane8 == 0, pltpu.roll(left, 1, 1), pltpu.roll(here, 1, 1))
        for ref, value in ((c_right, next_cell), (c_left, last_cell), (c_down, below)):
            ref[index] = 0.5 * (here + value)
        edge_left = jnp.where(lane8 < 2, pltpu.roll(left, 2, 1), pltpu.roll(here, 2, 1))
        edge_right = jnp.where(lane8 < 2, pltpu.roll(here, 2, 1), pltpu.roll(right, 2, 1))
        both = jnp.where(lane8 < 3, edge_left, pltpu.roll(edge_right, 2, 1))
        start = 6 * index
        inside = (lane8 >= start) & (lane8 < start + 6)
        gap_extra[...] = jnp.where(inside, pltpu.roll(both, start, 1), gap_extra[...])
        return carry

    def tables(steps, skip):
        lax.fori_loop(0, steps, functools.partial(coefficients, skip=skip), 0)
        slab = gap_extra[...]
        for n, shift in enumerate((LANES - 1, 1, LANES - 6, 6)):
            e_coef[n] = 0.5 * (slab + pltpu.roll(slab, shift, 1))

    gap_extra[...] = jnp.zeros((K, LANES), F32)
    tables(ROWS + 4, 0)

    for peer in group:
        extra_copy(peer, 0, peer).wait_recv()
        row_copy(peer, 0, 0, 2, CHUNKS, peer).wait_recv()

    lane32 = lane_iota(32)
    for n, shift in enumerate((LANES - 12, 32)):
        packed = jnp.zeros((32, LANES), F32)
        for g in range(8):
            moved = pltpu.roll(extra[0, 32 * g : 32 * g + 32, :], (shift + 16 * g) % LANES, 1)
            packed = jnp.where((lane32 >= 16 * g) & (lane32 < 16 * g + 16), moved, packed)
        halo_out[n] = packed

    edge_copies = [
        z_copy(halo_out.at[0], halo_in.at[1], 2, before),
        z_copy(halo_out.at[1], halo_in.at[0], 3, after),
        z_copy(rows_v.at[pl.ds(2, 2)], rows_v.at[pl.ds(ROWS + 2, 2)], 4, before),
        z_copy(rows_v.at[pl.ds(ROWS, 2)], rows_v.at[pl.ds(0, 2)], 5, after),
    ]

    def send_edges():
        for peer in group:
            row_copy(peer, 0, 14, 2, CHUNKS + 1, peer).wait_recv()
        for copy in gap_copies + edge_copies:
            copy.start()

    top, bottom = space == 0, space == count - 1

    def put(k, g, column, value):
        high, low = split(value)
        at = pl.ds(pl.multiple_of(k * MODES + g * 16, 16), 16)
        x_hi[at, column : column + LANES] = high
        x_lo[at, column : column + LANES] = low

    column = lax.rem(lane8[:1], 6)
    outside = ((column == 1) & (quarter == 0)) | ((column == 4) & (quarter == 3))

    def extra_terms(g, carry):
        v = extra[0, pl.ds(pl.multiple_of(g * 16, 16), 16), :]
        diffs = [v - pltpu.roll(v, shift, 1) for shift in (LANES - 1, 1, LANES - 6, 6)]
        for k in range(K):
            total = e_coef[0, k : k + 1, :] * diffs[0]
            for n in range(1, 4):
                total = total + e_coef[n, k : k + 1, :] * diffs[n]
            put(k, g, 0, total)
        return carry

    def take_edges():
        for copy in gap_copies + edge_copies:
            copy.wait_recv()

        @pl.when(jnp.logical_not(top))
        def _():
            gap_pad[0:2] = gap_halo[0]

        @pl.when(jnp.logical_not(bottom))
        def _():
            gap_pad[ROWS + 2 : ROWS + 4] = gap_halo[1]

        tables(5, ROWS - 1)

        @pl.when(top)
        def _():
            rows_v[0:2] = jnp.zeros((2, MODES, LANES), F32)

        @pl.when(bottom)
        def _():
            rows_v[ROWS + 2 : ROWS + 4] = jnp.zeros((2, MODES, LANES), F32)

        upper = jnp.where(top, 0.0, halo_in[0])
        lower = jnp.where(bottom, 0.0, halo_in[1])
        for g in range(8):
            at = slice(32 * g, 32 * g + 32)
            value = jnp.where(lane32 < 12, pltpu.roll(upper, (LANES - 16 * g) % LANES, 1), extra[0, at, :])
            inside = (lane32 >= 108) & (lane32 < 120)
            extra[0, at, :] = jnp.where(inside, pltpu.roll(lower, (108 - 16 * g) % LANES, 1), value)

    lane16 = lane_iota(16)

    def terms(base, side_index, index):
        for g in range(GROUPS):
            at = slice(g * 16, g * 16 + 16)
            v = [rows_v[base + n, at, :] for n in range(4)]
            side = extra[side_index, at, :]
            down = [v[n] - v[n + 1] for n in range(3)]
            diffs = []
            for n in range(2):
                here = v[n + 1]
                lane = 6 * (index + n)
                left = jnp.where(lane16 == 0, pltpu.roll(side, LANES - 1 - lane, 1), pltpu.roll(here, 1, 1))
                right = jnp.where(
                    lane16 == LANES - 1, pltpu.roll(side, LANES - 5 - lane, 1), pltpu.roll(here, LANES - 1, 1)
                )
                diffs.append((here - left, here - right))
            for k in range(K):
                flux = [c_down[index - 1 + n, k : k + 1, :] * down[n] for n in range(3)]
                for n in range(2):
                    total = (
                        c_left[index + n, k : k + 1, :] * diffs[n][0]
                        + c_right[index + n, k : k + 1, :] * diffs[n][1]
                    )
                    put(k, g, n * LANES, total + (flux[n + 1] - flux[n]))

    def home_copy(peer, owner_of_block, pair, their_quarter):
        return pltpu.make_async_remote_copy(
            src_ref=rows_v.at[pl.ds(DAMPED + 2 * pair, 2), pl.ds(pl.multiple_of(owner_of_block * BLOCK, BLOCK), BLOCK)],
            dst_ref=home.at[their_quarter, pl.ds(2 * pair, 2)],
            send_sem=out_send.at[pair, peer],
            recv_sem=out_recv.at[pair, their_quarter],
            device_id=(space, peer),
            device_id_type=MESH,
        )

    last = ROWS // 2

    def own_copy(pair):
        return pltpu.make_async_copy(
            rows_v.at[pl.ds(DAMPED + 2 * pair, 2), pl.ds(mine, BLOCK)], home.at[quarter, pl.ds(2 * pair, 2)], own_sem.at[pair]
        )

    again = 2 * last - 2

    def task(n, carry):
        is_extra = (n == 0) | (n == again)
        m = n - jnp.where(n > again, 1, 0)
        is_first = (m == 1) | (lax.rem(m, 2) == 0)
        f = lax.rem(jnp.where(m == 1, 1, m // 2 + 1), last + 1)
        d = lax.rem(jnp.maximum(m - 1, 0) // 2, last)
        base = jnp.where(is_first, 2 * f, FIRST + 2 * d)
        target = jnp.where(is_first, FIRST + 2 * f, DAMPED + 2 * d)
        target = jnp.where(is_extra, DAMPED + ROWS, target)
        index = jnp.where(is_first, 2 * f + 1, 2 * d + 2)

        @pl.when(jnp.logical_not(is_extra) & is_first & (f >= 1) & (f <= CHUNKS))
        def _():
            for peer in group:
                row_copy(peer, 0, 2 * f, 2, f - 1, peer).wait_recv()

        @pl.when((n == MEET) & is_gate)
        def _():
            meet_neighbours()

        @pl.when((n == MEET + 1) & is_gate)
        def _():
            pass_on()

        @pl.when((n == MEET + 2) & jnp.logical_not(is_gate))
        def _():
            pl.semaphore_wait(proceed, 1)

        @pl.when(n == MEET + 2)
        def _():
            send_edges()

        @pl.when(n == again)
        def _():
            take_edges()

        @pl.when(is_extra)
        def _():
            lax.fori_loop(0, GROUPS, extra_terms, 0, unroll=8)

        @pl.when(jnp.logical_not(is_extra))
        def _():
            terms(base, jnp.where(is_first, 0, 1), index)

        result = (
            jnp.dot(mix_hi[...], x_hi[...], preferred_element_type=F32)
            + jnp.dot(mix_hi[...], x_lo[...], preferred_element_type=F32)
            + jnp.dot(mix_lo[...], x_hi[...], preferred_element_type=F32)
        )
        rows_v[target] = jnp.where(is_first & (f == 0) & top, 0.0, result[:, :LANES])
        rows_v[target + 1] = jnp.where(is_first & (f == last) & bottom, 0.0, result[:, LANES:])

        @pl.when(is_extra)
        def _():
            extra[1] = jnp.where(outside, 0.0, rows_v[DAMPED + ROWS])

        @pl.when(jnp.logical_not(is_extra | is_first))
        def _():
            for peer in group:
                home_copy(peer, peer, d, quarter).start()
            own_copy(d).start()

        return carry

    lax.fori_loop(0, 2 * last + 3, task, 0)

    for pair in range(last):
        for peer, peer_quarter in zip(group, group_quarter):
            home_copy(peer, mode, pair, peer_quarter).wait_recv()
        own_copy(pair).wait()

    for slot, row in [(c, 2 * c + 2) for c in range(CHUNKS)] + [(CHUNKS, 0), (CHUNKS + 1, 14)]:
        for peer in group:
            row_copy(peer, 0, row, 2, slot, mode).wait_send()
    for peer in group:
        extra_copy(peer, 0, mode).wait_send()
        for pair in range(ROWS // 2):
            home_copy(peer, peer, pair, quarter).wait_send()
    for copy in gap_copies + edge_copies:
        copy.wait_send()


def arrange(home, out, taken, laid, load_sem, store_sem):
    rows = ROWS // 2
    places = [(n, t) for n in range(2) for t in range(4)]
    stores = [
        pltpu.make_async_copy(laid.at[n, t], out.at[:, n, :, t * LANES : (t + 1) * LANES], store_sem.at[n, t])
        for n, t in places
    ]
    loads = [
        pltpu.make_async_copy(home.at[t, pl.ds(n * rows, rows)], taken.at[n, t], load_sem.at[n, t]) for n, t in places
    ]
    for load in loads:
        load.start()
    for load, store, (n, t) in zip(loads, stores, places):
        load.wait()
        flat = laid.at[n, t].reshape(BLOCK * rows, LANES)
        for r in range(rows):
            flat[pl.ds(r, BLOCK, stride=rows), :] = taken[n, t, r]
        store.start()
    for store in stores:
        store.wait()


def per_device(pressure, gap_terms, coupling, pattern):
    cells = pressure.shape[2]
    vmem = pltpu.VMEM
    result = pl.pallas_call(
        kernel,
        out_shape=jax.ShapeDtypeStruct((4, ROWS, BLOCK, LANES), F32),
        in_specs=[
            pl.BlockSpec(memory_space=pl.ANY),
            pl.BlockSpec(memory_space=pl.ANY),
            pl.BlockSpec(memory_space=pl.ANY),
            pl.BlockSpec(memory_space=pl.ANY),
        ],
        out_specs=pl.BlockSpec(memory_space=pl.ANY),
        scratch_shapes=[
            vmem((4, BLOCK * ROWS, LANES), F32),
            vmem((4, K * ROWS, LANES), F32),
            vmem((K, MODES, MODES), F32),
            vmem((4, 4, K), jnp.int32),
            vmem((DAMPED + ROWS + 2, MODES, LANES), F32),
            vmem((2, MODES, LANES), F32),
            vmem((4, BLOCK, LANES), F32),
            vmem((4, ROWS, BLOCK, LANES), F32),
            vmem((ROWS + 4, K, cells + 2 * LANES), F32),
            vmem((ROWS + 4, K, LANES), F32),
            vmem((ROWS + 4, K, LANES), F32),
            vmem((ROWS + 4, K, LANES), F32),
            vmem((4, K, LANES), F32),
            vmem((MODES, K * MODES), BF16),
            vmem((MODES, K * MODES), BF16),
            vmem((K * MODES, 2 * LANES), BF16),
            vmem((K * MODES, 2 * LANES), BF16),
            vmem((2, 32, LANES), F32),
            vmem((2, 32, LANES), F32),
            vmem((2, 2, K, cells + 2 * LANES), F32),
            vmem((K, LANES), F32),
            pltpu.SemaphoreType.DMA((10,)),
            pltpu.SemaphoreType.DMA((CHUNKS + 3, 4)),
            pltpu.SemaphoreType.DMA((CHUNKS + 3, 4)),
            pltpu.SemaphoreType.DMA((6,)),
            pltpu.SemaphoreType.DMA((6,)),
            pltpu.SemaphoreType.DMA((ROWS // 2, 4)),
            pltpu.SemaphoreType.DMA((ROWS // 2, 4)),
            pltpu.SemaphoreType.DMA((ROWS // 2,)),
            pltpu.SemaphoreType.REGULAR,
            pltpu.SemaphoreType.REGULAR,
            pltpu.SemaphoreType.REGULAR,
        ],
        compiler_params=pltpu.CompilerParams(
            collective_id=0, has_side_effects=True, vmem_limit_bytes=56 * 1024 * 1024
        ),
        cost_estimate=pl.CostEstimate(flops=26_000_000_000, bytes_accessed=7_000_000, transcendentals=0),
        name="galerkin_twice",
    )(pressure.reshape(BLOCK * ROWS, cells), gap_terms.reshape(K * ROWS, cells), coupling, pattern.transpose(1, 2, 0))
    out = pl.pallas_call(
        arrange,
        out_shape=jax.ShapeDtypeStruct((BLOCK, 2, ROWS // 2, cells), F32),
        in_specs=[pl.BlockSpec(memory_space=pl.ANY)],
        out_specs=pl.BlockSpec(memory_space=pl.ANY),
        scratch_shapes=[
            vmem((2, 4, ROWS // 2, BLOCK, LANES), F32),
            vmem((2, 4, BLOCK, ROWS // 2, LANES), F32),
            pltpu.SemaphoreType.DMA((2, 4)),
            pltpu.SemaphoreType.DMA((2, 4)),
        ],
        compiler_params=pltpu.CompilerParams(vmem_limit_bytes=60 * 1024 * 1024),
        cost_estimate=pl.CostEstimate(flops=0, bytes_accessed=4_200_000, transcendentals=0),
        name="arrange",
    )(result)
    return out.reshape(pressure.shape)


def solution(mesh):
    placed = (P("modes", "space", None), P(None, "space", None), P(), P())
    return jax.shard_map(
        per_device, mesh=mesh, in_specs=placed, out_specs=P("modes", "space", None), check_vma=False
    )
```

```python
import functools

import jax
import jax.numpy as jnp
from jax import lax
from jax.experimental import pallas as pl
from jax.experimental.pallas import tpu as pltpu
from jax.sharding import PartitionSpec as P

MESH = pl.DeviceIdType.MESH
K = 8
MODES = 256
BLOCK = 64
ROWS = 16
LANES = 128
ZRUN = 8
GROUPS = MODES // 16
CHUNKS = 6
GATE = 3
MEET = 1
FIRST = ROWS + 4
DAMPED = 2 * ROWS + 6
F32 = jnp.float32
BF16 = jnp.bfloat16


def lane_iota(rows):
    return lax.broadcasted_iota(jnp.int32, (rows, LANES), 1)


def split(value):
    high = value.astype(BF16)
    return high, (value - high.astype(F32)).astype(BF16)


def kernel(
    press, gap, coupling, pattern, home,
    strip, gap_in, coup, pattern_in, rows_v, extra, extra_own, sendrows,
    gap_pad, c_right, c_left, c_down, e_coef, mix_hi, mix_lo, x_hi, x_lo, halo_out, halo_in, gap_halo, gap_extra,
    load_sem, in_send, in_recv, z_send, z_recv, out_send, out_recv, own_sem, entered, beside_in, proceed,
):
    space = lax.axis_index("space")
    mode = lax.axis_index("modes")
    count = lax.axis_size("space")
    y_lo = lax.rem(lax.div(space, ZRUN), 2)

    def swapped(index, bit):
        return index + bit * (lax.rem(index, 2) * 2 + lax.div(index, 2) - index)

    quarter = swapped(mode, y_lo)
    hi, core = lax.div(mode, 2), lax.rem(mode, 2)
    group = [(1 - hi) * 2 + core, (1 - hi) * 2 + 1 - core, hi * 2 + 1 - core]
    group_quarter = [swapped(peer, y_lo) for peer in group]

    def beside(step):
        other = lax.rem(space + step + count, count)
        other_y = lax.rem(lax.div(other, ZRUN), 2)
        return (other, swapped(quarter, other_y))

    before, after = beside(-1), beside(1)

    def columns(t):
        return slice(t * LANES, (t + 1) * LANES)

    press_loads = [pltpu.make_async_copy(press.at[:, columns(t)], strip.at[t], load_sem.at[t]) for t in range(4)]
    gap_loads = [pltpu.make_async_copy(gap.at[:, columns(t)], gap_in.at[t], load_sem.at[4 + t]) for t in range(4)]
    coup_load = pltpu.make_async_copy(coupling, coup, load_sem.at[8])
    pattern_load = pltpu.make_async_copy(pattern, pattern_in, load_sem.at[9])
    for load in press_loads + gap_loads + [coup_load, pattern_load]:
        load.start()

    is_gate = mode == GATE
    barrier = pltpu.get_barrier_semaphore()
    for peer in group:

        @pl.when(peer != GATE)
        def _():
            pl.semaphore_signal(barrier, inc=1, device_id=(space, peer), device_id_type=MESH)

    @pl.when(is_gate)
    def _():
        for peer in (before, after):
            pl.semaphore_signal(barrier, inc=1, device_id=peer, device_id_type=MESH)

    for load in press_loads:
        load.wait()

    def own_rows(g, carry):
        at = pl.ds(pl.multiple_of(g * 8, 8), 8)
        lane = lane_iota(8)
        parts = [jnp.zeros((8, LANES), F32) for _ in range(4)]
        for r in range(ROWS):
            start = 6 * (r + 2)
            inside = (lane >= start) & (lane < start + 4)
            for t in range(4):
                value = strip[t, pl.ds(g * (8 * ROWS) + r, 8, stride=ROWS), :]
                sendrows[t, r, at, :] = value
                parts[t] = jnp.where(inside, pltpu.roll(value, start + 2, 1), parts[t])
        nothing = jnp.zeros((8, LANES), F32)
        place = lax.rem(lane, 6)
        moved = [pltpu.roll(part, 2, 1) for part in parts] + [nothing]
        for t in range(4):
            left = parts[t - 1] if t else nothing
            value = jnp.where(place < 2, left, jnp.where(place == 2, parts[t], moved[t]))
            extra_own[t, at, :] = jnp.where(place < 4, value, moved[t + 1])
        return carry

    lax.fori_loop(0, BLOCK // 8, own_rows, 0)

    @pl.when(jnp.logical_not(is_gate))
    def _():
        pl.semaphore_wait(barrier, 3)
        pl.semaphore_signal(entered, inc=1, device_id=(space, GATE), device_id_type=MESH)

    @pl.when(is_gate)
    def _():
        pl.semaphore_wait(entered, 3)

    def meet_neighbours():
        pl.semaphore_wait(barrier, 2)
        for peer in (before, after):
            pl.semaphore_signal(beside_in, inc=1, device_id=peer, device_id_type=MESH)

    def pass_on():
        pl.semaphore_wait(beside_in, 2)
        for peer in group:
            pl.semaphore_signal(proceed, inc=1, device_id=(space, peer), device_id_type=MESH)

    mine = pl.multiple_of(mode * BLOCK, BLOCK)

    def row_copy(peer, peer_quarter, row, rows, slot, source):
        return pltpu.make_async_remote_copy(
            src_ref=sendrows.at[peer_quarter, pl.ds(row, rows)],
            dst_ref=rows_v.at[pl.ds(row + 2, rows), pl.ds(pl.multiple_of(source * BLOCK, BLOCK), BLOCK)],
            send_sem=in_send.at[slot, peer],
            recv_sem=in_recv.at[slot, source],
            device_id=(space, peer),
            device_id_type=MESH,
        )

    def extra_copy(peer, peer_quarter, source):
        return pltpu.make_async_remote_copy(
            src_ref=extra_own.at[peer_quarter],
            dst_ref=extra.at[0, pl.ds(pl.multiple_of(source * BLOCK, BLOCK), BLOCK)],
            send_sem=in_send.at[CHUNKS + 2, peer],
            recv_sem=in_recv.at[CHUNKS + 2, source],
            device_id=(space, peer),
            device_id_type=MESH,
        )

    for peer, peer_quarter in zip(group, group_quarter):
        extra_copy(peer, peer_quarter, mode).start()
    for row in (0, 14, 2, 4, 6, 8, 10, 12):
        slot = {0: CHUNKS, 14: CHUNKS + 1}.get(row, row // 2 - 1)
        for peer, peer_quarter in zip(group, group_quarter):
            row_copy(peer, peer_quarter, row, 2, slot, mode).start()

    for load in gap_loads:
        load.wait()
    for r in range(ROWS):
        slabs = [gap_in[t, pl.ds(r, K, stride=ROWS), :] for t in range(4)]
        slabs = [jnp.broadcast_to(slabs[0][:, :1], (K, LANES)), *slabs, jnp.broadcast_to(slabs[3][:, LANES - 1 :], (K, LANES))]
        for t in range(6):
            for place in {0: (0, 1, 2), ROWS - 1: (ROWS + 1, ROWS + 2, ROWS + 3)}.get(r, (r + 2,)):
                gap_pad[place, :, columns(t)] = slabs[t]

    def z_copy(source, target, slot, device):
        return pltpu.make_async_remote_copy(
            src_ref=source, dst_ref=target, send_sem=z_send.at[slot], recv_sem=z_recv.at[slot],
            device_id=device, device_id_type=MESH,
        )

    gap_copies = [
        z_copy(gap_pad.at[pl.ds(2, 2)], gap_halo.at[1], 0, before),
        z_copy(gap_pad.at[pl.ds(ROWS, 2)], gap_halo.at[0], 1, after),
    ]

    extra[0, pl.ds(mine, BLOCK), :] = extra_own[quarter]
    for r in range(ROWS):
        rows_v[r + 2, pl.ds(mine, BLOCK), :] = sendrows[quarter, r]

    coup_load.wait()
    pattern_load.wait()
    wide = lax.broadcasted_iota(jnp.int32, (1, MODES), 1)
    for k in range(K):
        for b in range(4):
            scale = [pattern_in[b, c : c + 1, k : k + 1].astype(F32) for c in range(4)]
            factor = jnp.where(
                wide < 128,
                jnp.where(wide < 64, scale[0], scale[1]),
                jnp.where(wide < 192, scale[2], scale[3]),
            )
            high, low = split(coup[k, b * BLOCK : (b + 1) * BLOCK, :] * factor)
            mix_hi[b * BLOCK : (b + 1) * BLOCK, k * MODES : (k + 1) * MODES] = high
            mix_lo[b * BLOCK : (b + 1) * BLOCK, k * MODES : (k + 1) * MODES] = low

    def tile(index, side):
        return gap_pad[index, :, pl.ds(pl.multiple_of((quarter + side) * LANES, LANES), LANES)]

    lane8 = lane_iota(8)

    def coefficients(step, carry, skip):
        index = step + jnp.where(step >= 2, skip, 0)
        left, here, right = tile(index, 0), tile(index, 1), tile(index, 2)
        below = tile(jnp.minimum(index + 1, ROWS + 3), 1)
        next_cell = jnp.where(lane8 == LANES - 1, pltpu.roll(right, LANES - 1, 1), pltpu.roll(here, LANES - 1, 1))
        last_cell = jnp.where(lane8 == 0, pltpu.roll(left, 1, 1), pltpu.roll(here, 1, 1))
        for ref, value in ((c_right, next_cell), (c_left, last_cell), (c_down, below)):
            ref[index] = 0.5 * (here + value)
        edge_left = jnp.where(lane8 < 2, pltpu.roll(left, 2, 1), pltpu.roll(here, 2, 1))
        edge_right = jnp.where(lane8 < 2, pltpu.roll(here, 2, 1), pltpu.roll(right, 2, 1))
        both = jnp.where(lane8 < 3, edge_left, pltpu.roll(edge_right, 2, 1))
        start = 6 * index
        inside = (lane8 >= start) & (lane8 < start + 6)
        gap_extra[...] = jnp.where(inside, pltpu.roll(both, start, 1), gap_extra[...])
        return carry

    def tables(steps, skip):
        lax.fori_loop(0, steps, functools.partial(coefficients, skip=skip), 0)
        slab = gap_extra[...]
        for n, shift in enumerate((LANES - 1, 1, LANES - 6, 6)):
            e_coef[n] = 0.5 * (slab + pltpu.roll(slab, shift, 1))

    gap_extra[...] = jnp.zeros((K, LANES), F32)
    tables(ROWS + 4, 0)

    for peer in group:
        extra_copy(peer, 0, peer).wait_recv()
        row_copy(peer, 0, 0, 2, CHUNKS, peer).wait_recv()

    lane32 = lane_iota(32)
    for n, shift in enumerate((LANES - 12, 32)):
        packed = jnp.zeros((32, LANES), F32)
        for g in range(8):
            moved = pltpu.roll(extra[0, 32 * g : 32 * g + 32, :], (shift + 16 * g) % LANES, 1)
            packed = jnp.where((lane32 >= 16 * g) & (lane32 < 16 * g + 16), moved, packed)
        halo_out[n] = packed

    edge_copies = [
        z_copy(halo_out.at[0], halo_in.at[1], 2, before),
        z_copy(halo_out.at[1], halo_in.at[0], 3, after),
        z_copy(rows_v.at[pl.ds(2, 2)], rows_v.at[pl.ds(ROWS + 2, 2)], 4, before),
        z_copy(rows_v.at[pl.ds(ROWS, 2)], rows_v.at[pl.ds(0, 2)], 5, after),
    ]

    def send_edges():
        for peer in group:
            row_copy(peer, 0, 14, 2, CHUNKS + 1, peer).wait_recv()
        for copy in gap_copies + edge_copies:
            copy.start()

    top, bottom = space == 0, space == count - 1

    def put(k, g, column, value):
        high, low = split(value)
        at = pl.ds(pl.multiple_of(k * MODES + g * 16, 16), 16)
        x_hi[at, column : column + LANES] = high
        x_lo[at, column : column + LANES] = low

    column = lax.rem(lane8[:1], 6)
    outside = ((column == 1) & (quarter == 0)) | ((column == 4) & (quarter == 3))

    def extra_terms(g, carry):
        v = extra[0, pl.ds(pl.multiple_of(g * 16, 16), 16), :]
        diffs = [v - pltpu.roll(v, shift, 1) for shift in (LANES - 1, 1, LANES - 6, 6)]
        for k in range(K):
            total = e_coef[0, k : k + 1, :] * diffs[0]
            for n in range(1, 4):
                total = total + e_coef[n, k : k + 1, :] * diffs[n]
            put(k, g, 0, total)
        return carry

    def take_edges():
        for copy in gap_copies + edge_copies:
            copy.wait_recv()

        @pl.when(jnp.logical_not(top))
        def _():
            gap_pad[0:2] = gap_halo[0]

        @pl.when(jnp.logical_not(bottom))
        def _():
            gap_pad[ROWS + 2 : ROWS + 4] = gap_halo[1]

        tables(5, ROWS - 1)

        @pl.when(top)
        def _():
            rows_v[0:2] = jnp.zeros((2, MODES, LANES), F32)

        @pl.when(bottom)
        def _():
            rows_v[ROWS + 2 : ROWS + 4] = jnp.zeros((2, MODES, LANES), F32)

        upper = jnp.where(top, 0.0, halo_in[0])
        lower = jnp.where(bottom, 0.0, halo_in[1])
        for g in range(8):
            at = slice(32 * g, 32 * g + 32)
            value = jnp.where(lane32 < 12, pltpu.roll(upper, (LANES - 16 * g) % LANES, 1), extra[0, at, :])
            inside = (lane32 >= 108) & (lane32 < 120)
            extra[0, at, :] = jnp.where(inside, pltpu.roll(lower, (108 - 16 * g) % LANES, 1), value)

    lane16 = lane_iota(16)

    def terms(base, side_index, index):
        for g in range(GROUPS):
            at = slice(g * 16, g * 16 + 16)
            v = [rows_v[base + n, at, :] for n in range(4)]
            side = extra[side_index, at, :]
            down = [v[n] - v[n + 1] for n in range(3)]
            diffs = []
            for n in range(2):
                here = v[n + 1]
                lane = 6 * (index + n)
                left = jnp.where(lane16 == 0, pltpu.roll(side, LANES - 1 - lane, 1), pltpu.roll(here, 1, 1))
                right = jnp.where(
                    lane16 == LANES - 1, pltpu.roll(side, LANES - 5 - lane, 1), pltpu.roll(here, LANES - 1, 1)
                )
                diffs.append((here - left, here - right))
            for k in range(K):
                flux = [c_down[index - 1 + n, k : k + 1, :] * down[n] for n in range(3)]
                for n in range(2):
                    total = (
                        c_left[index + n, k : k + 1, :] * diffs[n][0]
                        + c_right[index + n, k : k + 1, :] * diffs[n][1]
                    )
                    put(k, g, n * LANES, total + (flux[n + 1] - flux[n]))

    def home_copy(peer, owner_of_block, pair, their_quarter):
        return pltpu.make_async_remote_copy(
            src_ref=rows_v.at[pl.ds(DAMPED + 2 * pair, 2), pl.ds(pl.multiple_of(owner_of_block * BLOCK, BLOCK), BLOCK)],
            dst_ref=home.at[their_quarter, pl.ds(2 * pair, 2)],
            send_sem=out_send.at[pair, peer],
            recv_sem=out_recv.at[pair, their_quarter],
            device_id=(space, peer),
            device_id_type=MESH,
        )

    last = ROWS // 2

    def own_copy(pair):
        return pltpu.make_async_copy(
            rows_v.at[pl.ds(DAMPED + 2 * pair, 2), pl.ds(mine, BLOCK)], home.at[quarter, pl.ds(2 * pair, 2)], own_sem.at[pair]
        )

    again = 2 * last - 2

    def task(n, carry):
        is_extra = (n == 0) | (n == again)
        m = n - jnp.where(n > again, 1, 0)
        is_first = (m == 1) | (lax.rem(m, 2) == 0)
        f = lax.rem(jnp.where(m == 1, 1, m // 2 + 1), last + 1)
        d = lax.rem(jnp.maximum(m - 1, 0) // 2, last)
        base = jnp.where(is_first, 2 * f, FIRST + 2 * d)
        target = jnp.where(is_first, FIRST + 2 * f, DAMPED + 2 * d)
        target = jnp.where(is_extra, DAMPED + ROWS, target)
        index = jnp.where(is_first, 2 * f + 1, 2 * d + 2)

        @pl.when(jnp.logical_not(is_extra) & is_first & (f >= 1) & (f <= CHUNKS))
        def _():
            for peer in group:
                row_copy(peer, 0, 2 * f, 2, f - 1, peer).wait_recv()

        @pl.when((n == MEET) & is_gate)
        def _():
            meet_neighbours()

        @pl.when((n == MEET + 1) & is_gate)
        def _():
            pass_on()

        @pl.when((n == MEET + 2) & jnp.logical_not(is_gate))
        def _():
            pl.semaphore_wait(proceed, 1)

        @pl.when(n == MEET + 2)
        def _():
            send_edges()

        @pl.when(n == again)
        def _():
            take_edges()

        @pl.when(is_extra)
        def _():
            lax.fori_loop(0, GROUPS, extra_terms, 0, unroll=8)

        @pl.when(jnp.logical_not(is_extra))
        def _():
            terms(base, jnp.where(is_first, 0, 1), index)

        result = (
            jnp.dot(mix_hi[...], x_hi[...], preferred_element_type=F32)
            + jnp.dot(mix_hi[...], x_lo[...], preferred_element_type=F32)
            + jnp.dot(mix_lo[...], x_hi[...], preferred_element_type=F32)
        )
        rows_v[target] = jnp.where(is_first & (f == 0) & top, 0.0, result[:, :LANES])
        rows_v[target + 1] = jnp.where(is_first & (f == last) & bottom, 0.0, result[:, LANES:])

        @pl.when(is_extra)
        def _():
            extra[1] = jnp.where(outside, 0.0, rows_v[DAMPED + ROWS])

        @pl.when(jnp.logical_not(is_extra | is_first))
        def _():
            for peer in group:
                home_copy(peer, peer, d, quarter).start()
            own_copy(d).start()

        return carry

    lax.fori_loop(0, 2 * last + 3, task, 0)

    for pair in range(last):
        for peer, peer_quarter in zip(group, group_quarter):
            home_copy(peer, mode, pair, peer_quarter).wait_recv()
        own_copy(pair).wait()

    for slot, row in [(c, 2 * c + 2) for c in range(CHUNKS)] + [(CHUNKS, 0), (CHUNKS + 1, 14)]:
        for peer in group:
            row_copy(peer, 0, row, 2, slot, mode).wait_send()
    for peer in group:
        extra_copy(peer, 0, mode).wait_send()
        for pair in range(ROWS // 2):
            home_copy(peer, peer, pair, quarter).wait_send()
    for copy in gap_copies + edge_copies:
        copy.wait_send()


def arrange(home, out, taken, laid, load_sem, store_sem):
    rows = ROWS // 2
    places = [(n, t) for n in range(2) for t in range(4)]
    stores = [
        pltpu.make_async_copy(laid.at[n, t], out.at[:, n, :, t * LANES : (t + 1) * LANES], store_sem.at[n, t])
        for n, t in places
    ]
    loads = [
        pltpu.make_async_copy(home.at[t, pl.ds(n * rows, rows)], taken.at[n, t], load_sem.at[n, t]) for n, t in places
    ]
    for load in loads:
        load.start()
    for load, store, (n, t) in zip(loads, stores, places):
        load.wait()
        flat = laid.at[n, t].reshape(BLOCK * rows, LANES)
        for r in range(rows):
            flat[pl.ds(r, BLOCK, stride=rows), :] = taken[n, t, r]
        store.start()
    for store in stores:
        store.wait()


def per_device(pressure, gap_terms, coupling, pattern):
    cells = pressure.shape[2]
    vmem = pltpu.VMEM
    result = pl.pallas_call(
        kernel,
        out_shape=jax.ShapeDtypeStruct((4, ROWS, BLOCK, LANES), F32),
        in_specs=[
            pl.BlockSpec(memory_space=pl.ANY),
            pl.BlockSpec(memory_space=pl.ANY),
            pl.BlockSpec(memory_space=pl.ANY),
            pl.BlockSpec(memory_space=pl.ANY),
        ],
        out_specs=pl.BlockSpec(memory_space=pl.ANY),
        scratch_shapes=[
            vmem((4, BLOCK * ROWS, LANES), F32),
            vmem((4, K * ROWS, LANES), F32),
            vmem((K, MODES, MODES), F32),
            vmem((4, 4, K), jnp.int32),
            vmem((DAMPED + ROWS + 2, MODES, LANES), F32),
            vmem((2, MODES, LANES), F32),
            vmem((4, BLOCK, LANES), F32),
            vmem((4, ROWS, BLOCK, LANES), F32),
            vmem((ROWS + 4, K, cells + 2 * LANES), F32),
            vmem((ROWS + 4, K, LANES), F32),
            vmem((ROWS + 4, K, LANES), F32),
            vmem((ROWS + 4, K, LANES), F32),
            vmem((4, K, LANES), F32),
            vmem((MODES, K * MODES), BF16),
            vmem((MODES, K * MODES), BF16),
            vmem((K * MODES, 2 * LANES), BF16),
            vmem((K * MODES, 2 * LANES), BF16),
            vmem((2, 32, LANES), F32),
            vmem((2, 32, LANES), F32),
            vmem((2, 2, K, cells + 2 * LANES), F32),
            vmem((K, LANES), F32),
            pltpu.SemaphoreType.DMA((10,)),
            pltpu.SemaphoreType.DMA((CHUNKS + 3, 4)),
            pltpu.SemaphoreType.DMA((CHUNKS + 3, 4)),
            pltpu.SemaphoreType.DMA((6,)),
            pltpu.SemaphoreType.DMA((6,)),
            pltpu.SemaphoreType.DMA((ROWS // 2, 4)),
            pltpu.SemaphoreType.DMA((ROWS // 2, 4)),
            pltpu.SemaphoreType.DMA((ROWS // 2,)),
            pltpu.SemaphoreType.REGULAR,
            pltpu.SemaphoreType.REGULAR,
            pltpu.SemaphoreType.REGULAR,
        ],
        compiler_params=pltpu.CompilerParams(
            collective_id=0, has_side_effects=True, vmem_limit_bytes=56 * 1024 * 1024
        ),
        cost_estimate=pl.CostEstimate(flops=26_000_000_000, bytes_accessed=7_000_000, transcendentals=0),
        name="galerkin_twice",
    )(pressure.reshape(BLOCK * ROWS, cells), gap_terms.reshape(K * ROWS, cells), coupling, pattern.transpose(1, 2, 0))
    out = pl.pallas_call(
        arrange,
        out_shape=jax.ShapeDtypeStruct((BLOCK, 2, ROWS // 2, cells), F32),
        in_specs=[pl.BlockSpec(memory_space=pl.ANY)],
        out_specs=pl.BlockSpec(memory_space=pl.ANY),
        scratch_shapes=[
            vmem((2, 4, ROWS // 2, BLOCK, LANES), F32),
            vmem((2, 4, BLOCK, ROWS // 2, LANES), F32),
            pltpu.SemaphoreType.DMA((2, 4)),
            pltpu.SemaphoreType.DMA((2, 4)),
        ],
        compiler_params=pltpu.CompilerParams(vmem_limit_bytes=60 * 1024 * 1024),
        cost_estimate=pl.CostEstimate(flops=0, bytes_accessed=4_200_000, transcendentals=0),
        name="arrange",
    )(result)
    return out.reshape(pressure.shape)


def solution(mesh):
    placed = (P("modes", "space", None), P(None, "space", None), P(), P())
    return jax.shard_map(
        per_device, mesh=mesh, in_specs=placed, out_specs=P("modes", "space", None), check_vma=False
    )
```
